32 devices in a mesh: grp: 2 (over x), date: 16 (over z, y, core).
Axes of the slice: x: 2, y: 2, z: 4, core: 2. Of those that a mesh axis runs over, the one named last changes fastest.
Arguments:
- radar_stack: bfloat16 [2, 128, 256, 256], P(None, 'date', 'grp'), parts along dimension 2, may hold values from -6 to 6
- filter_taps: float32 [2, 128, 128], P(None, 'date'), may hold values from -0.6 to 0.6
- filter_lengths: int32 [128], P('date'), may hold values from 64 to 128
- resample_kernel: float32 [4], replicated, may hold values from 0.2 to 1
- tile_owner: int32 [512, 1], P(('grp', 'date')), parts along dimension 0, may hold values from 0 to 15; in each aligned block of 16 rows (0 to 15, 16 to 31, ...) at most 2 rows name the same one
- map_slot: int32 [512], P(('grp', 'date')), parts along dimension 0, may hold values from 0 to 7
- correlation: int32 [512], P(('grp', 'date')), parts along dimension 0, may hold values from 1 to 128
- offsets: int32 [512], P(('grp', 'date')), parts along dimension 0, may hold values from 0 to 127
Outputs:
- geocoded: float32 [256, 256, 128], P(('grp', 'date')), parts along dimension 0
The draws below stay inside these ranges and needn't reach their ends.
There are 2 independent parts, one for each index of `grp`. The reference program is written for one: setup_inputs(seed, part) draws one part's arguments, and reference() takes and returns one part's arrays. A program takes and returns all parts, laid end to end along the dimension named above; an argument that names none is the same for every part. Nothing has to cross between parts.
Inputs may be any that keep to these rules, and one draw needn't show every extreme that they name: `tile_owner`: among the 16 tiles of one device, at most 2 name the same owner.
All inputs are finite; a program needn't handle non-finite values. Where the reference program divides by a largest or mean magnitude, that divisor is 1e-20 or more.
Results may differ from the reference program's by a relative error of at most 0.0055.
Values may be sent and summed in bfloat16 or wider, within the bound.
No kernel may reach another device: no remote copies, remote signals or barrier semaphores. Data moves between devices by JAX's collectives and lax.ppermute only.
A program may use at most 64 MiB of HBM per device.

```python
import math
import jax
import jax.numpy as jnp
import numpy as np
from jax import lax

DATES = 128
TAPS = 128
RG = 256
PATCH_AZ = 8
PATCH_RG = 16
SWEEPS = 3
TILE = 128
KW = 4
CAP = 2
MAP_DEV = 8
AZ = 128
TILES_DEV = 16
TILES = 256
MAP_TILES = 128
N_DATE = 16


def place_ends(array, key, least, largest):
    extent = array.shape
    index_at = [jax.random.randint(jax.random.fold_in(key, axis), (), 0, extent[axis]) for axis in range(len(extent))]
    array = array.at[tuple(index_at)].set(least)
    longest = extent.index(max(extent))
    index_at[longest] = (index_at[longest] + 1) % extent[longest]
    return array.at[tuple(index_at)].set(largest)


def level_of(stream_key, extent, shards, smallest, largest):
    loudness, own = 1.0, jax.random.fold_in(stream_key, 6)
    for dim, shards_of in shards:
        draws = jnp.exp(jax.random.uniform(jax.random.fold_in(own, dim), (shards_of,), jnp.float32, smallest / len(shards), largest / len(shards)))
        loudness = loudness * jnp.repeat(draws, extent[dim] // shards_of).reshape([-1 if axis == dim else 1 for axis in range(len(extent))])
    return loudness


def assign_block(own_key, own, number, rows, amount, top, most, slope):
    ranking = jax.random.permutation(own_key, amount)
    packed, common = shares(amount, rows * top, most, slope, True), shares(amount, rows * top, most, slope, False)
    places = jnp.arange(amount)

    def named(sizes, turn):
        used = int((sizes > 0).sum())
        fixed = max(1, used // 4)
        passed = fixed + (places - fixed + turn * (used - fixed)) % max(1, amount - fixed)
        return jnp.zeros((amount,), jnp.int32).at[ranking[jnp.where(places < fixed, places, passed)]].set(jnp.asarray(sizes, jnp.int32))

    sizes = jnp.where(number % 4 == 0, named(packed, number // 4), named(common, number - number // 4 - 1))
    mixed = jax.random.permutation(jax.random.fold_in(own, 3), amount)
    source_of, taker = mixed[0:amount // 2 * 2:2], mixed[1:amount // 2 * 2:2]
    room = jnp.minimum(sizes[source_of] - 1, most - sizes[taker]) // 2
    room = jnp.where((source_of == ranking[0]) | (taker == ranking[0]) | (sizes[taker] == 0), 0, jnp.maximum(room, 0))
    passed = jax.random.randint(jax.random.fold_in(own, 4), (amount // 2,), 0, 1 << 20) % (room + 1)
    sizes = sizes.at[source_of].add(-passed).at[taker].add(passed)
    items = jnp.searchsorted(jnp.cumsum(sizes), jnp.arange(rows * top), side="right").astype(jnp.int32)
    listing = items.reshape(top, rows).T
    listing = listing[jax.random.permutation(jax.random.fold_in(own, 1), rows)]
    turn = jax.random.randint(jax.random.fold_in(own, 2), (rows, 1), 0, top)
    return jnp.take_along_axis(listing, (jnp.arange(top)[None, :] + turn) % top, axis=1)


def shares(number_of, total, reach, lean, full):
    loads = [(1 << 20) // math.isqrt(rank ** lean) + 1 for rank in range(1, number_of + 1)]
    largest = reach if full else min(reach, max(-(-total // number_of), total * loads[0] // sum(loads)))
    least = 1 if total - largest >= number_of - 1 else 0
    given, rest = [largest] + [least] * (number_of - 1), total - largest - least * (number_of - 1)
    while rest > 0:
        candidates = [i for i in range(1, number_of) if given[i] < largest] or [i for i in range(1, number_of) if given[i] < reach]
        mass, remaining = sum([loads[i] for i in candidates]), rest
        for i in candidates:
            more = min(reach - given[i], max(1, remaining * loads[i] // mass), rest)
            given[i] = given[i] + more
            rest = rest - more
    return np.array(given)


def gaussian(key, shape, scale, bound, cuts=(), kind=jnp.bfloat16):
    drawn = scale * jax.random.normal(key, shape, jnp.float32)
    if cuts:
        drawn = drawn * level_of(key, shape, cuts, -0.22, 0.18)
    return jnp.clip(drawn, -bound, bound).astype(kind)


def setup_inputs(seed: int = 0, part: int = 0) -> dict:
    streams_of = jax.random.split(jax.random.key(seed), 9)
    part_keys = jax.random.split(jax.random.fold_in(streams_of[8], part), 9)
    radar_stack = gaussian(part_keys[0], (2, DATES, AZ, RG), 1.0, 6.0, ((1, 16),))
    filter_taps = gaussian(streams_of[1], (2, DATES, TAPS), 0.1, 0.6, ((1, 16),), jnp.float32)
    filter_lengths = place_ends(jax.random.randint(streams_of[2], (DATES,), TAPS // 2, TAPS + 1), jax.random.fold_in(streams_of[2], 1), TAPS // 2, TAPS).astype(jnp.int32)
    resample_kernel = jnp.clip(jax.random.uniform(streams_of[3], (KW,), jnp.float32, 0.2, 1.0), 0.2, 1.0)
    tile_owner_keys = jax.random.split(jax.random.fold_in(part_keys[4], 1), TILES // TILES_DEV)
    tile_owner_turns = jax.random.permutation(jax.random.fold_in(part_keys[4], 3), TILES // TILES_DEV)
    tile_owner = jax.vmap(lambda own, number: assign_block(jax.random.fold_in(part_keys[4], 2), own, number, TILES_DEV, N_DATE, 1, CAP, 2))(tile_owner_keys, tile_owner_turns).reshape((TILES, 1))
    map_slot = place_ends(jax.random.randint(part_keys[5], (TILES,), 0, MAP_DEV), jax.random.fold_in(part_keys[5], 1), 0, MAP_DEV - 1).astype(jnp.int32)
    correlation = place_ends(jax.random.randint(part_keys[6], (TILES,), 1, TILE + 1), jax.random.fold_in(part_keys[6], 1), 1, TILE).astype(jnp.int32)
    offsets = place_ends(jax.random.randint(part_keys[7], (TILES,), 0, TILE), jax.random.fold_in(part_keys[7], 1), 0, TILE - 1).astype(jnp.int32)
    return {"radar_stack": radar_stack, "filter_taps": filter_taps, "filter_lengths": filter_lengths, "resample_kernel": resample_kernel, "tile_owner": tile_owner, "map_slot": map_slot, "correlation": correlation, "offsets": offsets}


diag_load = 0.5
small_eps = 1e-05
highest = lax.Precision.HIGHEST

def toeplitz_matrix(taps_one, length_one, rows_count):
    positions = jnp.arange(TAPS, dtype=jnp.int32)
    masked = jnp.where(positions < length_one, taps_one, jnp.zeros_like(taps_one))
    period = 2 * rows_count - 1
    padded = jnp.pad(masked, (0, period - TAPS))
    wrapped = jnp.roll(padded, -(TAPS // 2))
    flat_rows = jnp.tile(wrapped, rows_count)[:rows_count * (period - 1)]
    return flat_rows.reshape(rows_count, period - 1)[:, :rows_count]

def block_operator(taps_date, length_one, rows_count):
    real_mat = toeplitz_matrix(taps_date[0], length_one, rows_count)
    imag_mat = toeplitz_matrix(taps_date[1], length_one, rows_count)
    upper = jnp.concatenate([real_mat, -imag_mat], axis=1)
    lower = jnp.concatenate([imag_mat, real_mat], axis=1)
    return jnp.concatenate([upper, lower], axis=0).astype(jnp.bfloat16)

def complex_product(left_re, left_im, right_re, right_im):

    def mult(first, second):
        return jnp.einsum('pij,pjk->pik', first, second, precision=highest)
    return (mult(left_re, right_re) - mult(left_im, right_im), mult(left_re, right_im) + mult(left_im, right_re))

def whiten_patches(patches):
    values = patches.astype(jnp.float32)
    z_re = values[:, 0]
    z_im = values[:, 1]
    date_count = patches.shape[2]
    look_count = patches.shape[3]
    gram_re = (jnp.einsum('pil,pjl->pij', z_re, z_re, precision=highest) + jnp.einsum('pil,pjl->pij', z_im, z_im, precision=highest)) / look_count
    gram_im = (jnp.einsum('pil,pjl->pij', z_im, z_re, precision=highest) - jnp.einsum('pil,pjl->pij', z_re, z_im, precision=highest)) / look_count
    diagonal = jnp.diagonal(gram_re, axis1=1, axis2=2)
    scaled = lax.rsqrt(diagonal + small_eps)
    outer_scale = scaled[:, :, None] * scaled[:, None, :]
    identity = jnp.eye(date_count, dtype=jnp.float32)
    coher_re = gram_re * outer_scale + diag_load * identity[None]
    coher_im = gram_im * outer_scale
    row_bound = lax.optimization_barrier(jnp.max(lax.optimization_barrier(jnp.sum(jnp.abs(coher_re) + jnp.abs(coher_im), axis=2)), axis=1))
    inverse_re = identity[None] / row_bound[:, None, None]
    inverse_im = jnp.zeros_like(coher_im)
    for _ in range(SWEEPS):
        prod_re, prod_im = complex_product(coher_re, coher_im, inverse_re, inverse_im)
        corr_re, corr_im = complex_product(inverse_re, inverse_im, prod_re, prod_im)
        inverse_re = 2.0 * inverse_re - corr_re
        inverse_im = 2.0 * inverse_im - corr_im
    white_re, white_im = complex_product(inverse_re, inverse_im, z_re, z_im)
    return jnp.stack([white_re, white_im], axis=1).astype(jnp.bfloat16)

def to_patches(field):
    date_count = field.shape[1]
    rows_count = field.shape[2]
    ranges_count = field.shape[3]
    blocks = field.reshape(2, date_count, rows_count // PATCH_AZ, PATCH_AZ, ranges_count // PATCH_RG, PATCH_RG)
    return blocks.transpose(2, 4, 0, 1, 3, 5).reshape(-1, 2, date_count, PATCH_AZ * PATCH_RG)

def from_patches(patches, rows_count, ranges_count):
    date_count = patches.shape[2]
    blocks = patches.reshape(rows_count // PATCH_AZ, ranges_count // PATCH_RG, 2, date_count, PATCH_AZ, PATCH_RG)
    return blocks.transpose(2, 3, 0, 4, 1, 5).reshape(2, date_count, rows_count, ranges_count)

def to_tiles(field):
    date_count = field.shape[1]
    rows_count = field.shape[2]
    ranges_count = field.shape[3]
    blocks = field.reshape(2, date_count, rows_count, ranges_count // TILE, TILE)
    return blocks.transpose(2, 3, 0, 1, 4).reshape(-1, 2 * date_count, TILE)

def resample_tiles(tiles, shifts, resample_kernel):
    rounded = lax.optimization_barrier(resample_kernel.astype(jnp.bfloat16)).astype(jnp.float32)
    column = jnp.arange(TILE, dtype=jnp.int32)
    first_cell = column[None, :] + shifts.astype(jnp.int32)[:, None]
    matrix = jnp.zeros((shifts.shape[0], TILE, TILE), jnp.float32)
    for tap_index in range(KW):
        source = (first_cell + tap_index) % TILE
        matrix = matrix + rounded[tap_index] * (column[None, None, :] == source[:, :, None]).astype(jnp.float32)
    return jnp.einsum('sji,sci->scj', matrix, tiles.astype(jnp.float32), precision=highest)

def reference(radar_stack, filter_taps, filter_lengths, resample_kernel, tile_owner, map_slot, correlation, offsets):
    rows_count = radar_stack.shape[2]
    ranges_count = radar_stack.shape[3]

    def filter_one(operands):
        taps_date, length_one, columns = operands
        operator = block_operator(taps_date, length_one, rows_count).astype(jnp.float32)
        flat_cols = columns.reshape(2 * rows_count, ranges_count).astype(jnp.float32)
        product = jnp.dot(operator, flat_cols, precision=highest)
        return product.reshape(2, rows_count, ranges_count).astype(jnp.bfloat16)
    filtered = lax.map(filter_one, (filter_taps.transpose(1, 0, 2), filter_lengths, radar_stack.transpose(1, 0, 2, 3)))
    filtered = filtered.transpose(1, 0, 2, 3)
    patches = to_patches(filtered)
    grouped = patches.reshape((N_DATE, -1) + patches.shape[1:])
    whitened = lax.map(whiten_patches, grouped).reshape(patches.shape)
    field = from_patches(whitened, rows_count, ranges_count)
    tiles = to_tiles(field)
    tile_count = tiles.shape[0]
    resampled = resample_tiles(tiles, offsets, resample_kernel).reshape(tile_count, -1)
    targets = tile_owner[:, 0] * MAP_DEV + map_slot
    map_iota = jnp.arange(MAP_TILES, dtype=jnp.int32)
    spread = jnp.where(targets[None, :] == map_iota[:, None], correlation.astype(jnp.float32)[None, :], jnp.zeros((), jnp.float32))
    total = jnp.dot(spread, resampled, precision=highest)
    denominator = jnp.maximum(lax.optimization_barrier(jnp.sum(spread, axis=1)), 1.0)
    return (total / denominator[:, None]).reshape(MAP_TILES, 2 * DATES, TILE)
```

```python
from functools import partial

import jax
import jax.numpy as jnp
from jax import lax
from jax.experimental import pallas as pl
from jax.experimental.pallas import tpu as pltpu
from jax.sharding import PartitionSpec as P

PATCH_AZ = 8
PATCH_RG = 16
TILE = 128
KW = 4
CAP = 2
MAP_DEV = 8
GROUP = 4

diag_load = 0.5
small_eps = 1e-05
VMEM = pl.BlockSpec(memory_space=pltpu.VMEM)
SMEM = pl.BlockSpec(memory_space=pltpu.SMEM)
params = pltpu.CompilerParams(vmem_limit_bytes=48 * 1024 * 1024)


def filter_kernel(lengths, taps, radar, sent, staged):
    _, dates_here, rows_count, ranges_count = radar.shape
    tap_count = taps.shape[2]
    period = rows_count + tap_count
    position = lax.broadcasted_iota(jnp.int32, (1, tap_count), 1)
    for date in range(dates_here):
        mats = []
        for part in range(2):
            used = jnp.where(position < lengths[date], taps[part, pl.ds(date, 1), :], 0.0)
            padded = jnp.concatenate([used, jnp.zeros((1, period - tap_count), jnp.float32)], axis=1)
            spread = jnp.broadcast_to(padded, (rows_count, period))
            rolled = pltpu.roll(spread, period - tap_count // 2, 1, stride=1, stride_axis=0)
            mats.append(rolled[:, :rows_count])
        real_mat, imag_mat = mats
        columns = radar[:, date].reshape(2 * rows_count, ranges_count)
        for part, halves in enumerate(((real_mat, -imag_mat), (imag_mat, real_mat))):
            operator = jnp.concatenate(halves, axis=1).astype(jnp.bfloat16)
            product = jnp.dot(operator, columns, preferred_element_type=jnp.float32)
            for side in range(ranges_count // TILE):
                skewed = pltpu.roll(
                    product[:, side * TILE : (side + 1) * TILE], 0, 1, stride=PATCH_RG, stride_axis=0
                )
                first = part * dates_here + date
                staged[side, pl.ds(first, rows_count, stride=2 * dates_here), :] = skewed
    for side in range(ranges_count // TILE):
        sent[:, side * TILE : (side + 1) * TILE] = staged[side].astype(jnp.bfloat16)


def barrel(blocks, lane_block):
    count = len(blocks)
    step = 1
    while step < count:
        taken = (lane_block & step) != 0
        blocks = [jnp.where(taken, blocks[(i + step) % count], blocks[i]) for i in range(count)]
        step *= 2
    return blocks


def embedded(real_part, imag_part):
    upper = jnp.concatenate([real_part, -imag_part], axis=1)
    lower = jnp.concatenate([imag_part, real_part], axis=1)
    return jnp.concatenate([upper, lower], axis=0)


def whiten_group(cells):
    dates, looks = cells[0].shape[0] // 2, cells[0].shape[1]
    row = lax.broadcasted_iota(jnp.int32, (dates, dates), 0)
    col = lax.broadcasted_iota(jnp.int32, (dates, dates), 1)
    diagonal = row == col
    grams = []
    for cell in cells:
        real_part, imag_part = cell[:dates], cell[dates:]
        straight = jnp.concatenate([real_part, imag_part], axis=1)
        turned = jnp.concatenate([imag_part, -real_part], axis=1)
        left = jnp.concatenate([straight, turned], axis=0)
        grams.append(
            lax.dot_general(left, straight, (((1,), (1,)), ((), ())), preferred_element_type=jnp.float32)
        )
    scaled, bounds = [], []
    for gram in grams:
        gram_re, gram_im = gram[:dates], gram[dates:]
        power = jnp.where(diagonal, gram_re, 0.0)
        row_scale = lax.rsqrt(jnp.sum(power, axis=1, keepdims=True) * (1.0 / looks) + small_eps)
        col_scale = lax.rsqrt(jnp.sum(power, axis=0, keepdims=True) * (1.0 / looks) + small_eps)
        col_scale = col_scale * (1.0 / looks)
        size = (jnp.abs(gram_re) + jnp.abs(gram_im)) * row_scale
        sums = jnp.sum(size, axis=0, keepdims=True) * col_scale + diag_load
        inv_bound = 1.0 / jnp.max(sums, axis=1, keepdims=True)
        factor = row_scale * (col_scale * inv_bound)
        load = jnp.where(diagonal, diag_load * inv_bound, 0.0)
        scaled.append(jnp.concatenate([gram_re * factor + load, gram_im * factor], axis=0))
        bounds.append(inv_bound)
    values = [cell.astype(jnp.float32) for cell in cells]
    rounded = list(cells)
    for sweep in range(2):
        mats = [s.astype(jnp.bfloat16) for s in scaled]
        products = [
            jnp.dot(
                embedded(m[:dates], m[dates:]),
                jnp.concatenate([m, r], axis=1),
                preferred_element_type=jnp.float32,
            )
            for m, r in zip(mats, rounded)
        ]
        scaled = [2.0 * s - p[:, :dates] for s, p in zip(scaled, products)]
        values = [2.0 * v - p[:, dates:] for v, p in zip(values, products)]
        rounded = [v.astype(jnp.bfloat16) for v in values]
    mats = [s.astype(jnp.bfloat16) for s in scaled]
    products = [
        jnp.dot(embedded(m[:dates], m[dates:]), r, preferred_element_type=jnp.float32)
        for m, r in zip(mats, rounded)
    ]
    return [
        ((2.0 * v - p) * b).astype(jnp.bfloat16) for v, p, b in zip(values, products, bounds)
    ]


def whiten_kernel(slots, lines, packed, windows, *, mixed):
    senders, line_count, part_rows, ranges_count = lines.shape
    dates = windows.shape[1] // 2
    sides = ranges_count // TILE
    lane_block = lax.broadcasted_iota(jnp.int32, (1, TILE), 1) // PATCH_RG
    per_side = TILE // PATCH_RG
    for side in range(sides):
        lanes = pl.ds(side * TILE, TILE)
        if mixed:
            half = part_rows // 2
            for first in range(0, senders, 2):
                blocks = [
                    lines[first : first + 2, a, :, lanes].astype(jnp.float32) for a in range(line_count)
                ]
                found = barrel(blocks, lane_block[:, None])
                rows = pl.ds(first * half, 2 * half)
                rows_im = pl.ds(dates + first * half, 2 * half)
                for w in range(per_side):
                    block = found[-w % per_side]
                    real_part = block[:, :half].reshape(2 * half, TILE)
                    imag_part = block[:, half:].reshape(2 * half, TILE)
                    windows[side * per_side + w, rows, :] = real_part.astype(jnp.bfloat16)
                    windows[side * per_side + w, rows_im, :] = imag_part.astype(jnp.bfloat16)
        else:
            for first in range(0, 2 * dates, 16):
                rows = pl.ds(first, 16)
                blocks = [lines[0, a, rows, lanes].astype(jnp.float32) for a in range(line_count)]
                found = barrel(blocks, lane_block)
                for w in range(per_side):
                    windows[side * per_side + w, rows, :] = found[-w % per_side].astype(jnp.bfloat16)

    def group_step(step, carry):
        first = step * GROUP
        results = whiten_group([windows[first + k] for k in range(GROUP)])
        for k in range(GROUP):
            windows[first + k] = results[k]
        return carry

    lax.fori_loop(0, windows.shape[0] // GROUP, group_step, 0)
    for side in range(sides):
        for first in range(0, 2 * dates, 16):
            rows = pl.ds(first, 16)
            blocks = [
                windows[side * per_side + w, rows, :].astype(jnp.float32) for w in range(per_side)
            ]
            found = barrel(blocks, lane_block)
            for a in range(line_count):
                packed[slots[a * sides + side], rows, :] = found[-a % per_side].astype(jnp.bfloat16)


def map_kernel(order, targets, starts, count, kernel, scales, got, out, circulant):
    source = lax.broadcasted_iota(jnp.int32, circulant.shape, 0)
    column = lax.broadcasted_iota(jnp.int32, circulant.shape, 1)
    lag = (source - column) & (TILE - 1)
    taps = jnp.zeros(circulant.shape, jnp.float32)
    for k in range(KW):
        taps = jnp.where(lag == k, kernel[k], taps)
    circulant[...] = taps
    out[...] = jnp.zeros(out.shape, jnp.float32)

    def pair_step(step, carry):
        products = []
        for k in range(2):
            at = step * 2 + k
            matrix = circulant[pl.ds(starts[at], TILE), :].astype(jnp.bfloat16)
            products.append(
                jnp.dot(got[order[at]], matrix, preferred_element_type=jnp.float32) * scales[at]
            )
        for k in range(2):
            target = targets[step * 2 + k]
            out[target] = out[target] + products[k]
        return carry

    lax.fori_loop(0, (count[0] + 1) // 2, pair_step, 0)


def shards(
    radar_stack,
    filter_taps,
    filter_lengths,
    resample_kernel,
    tile_owner,
    map_slot,
    correlation,
    offsets,
):
    peers = lax.axis_size("date")
    me = lax.axis_index("date")
    _, dates_here, rows_count, ranges_count = radar_stack.shape
    dates = dates_here * peers
    line_count = rows_count // peers
    sides = ranges_count // TILE
    tile_count = line_count * sides
    slot_count = peers * CAP
    window_count = (line_count // PATCH_AZ) * (ranges_count // PATCH_RG)
    assert line_count == PATCH_AZ

    owners = tile_owner[:, 0]
    tile_iota = jnp.arange(tile_count, dtype=jnp.int32)
    starts_here = offsets + PATCH_RG * (tile_iota // sides)
    earlier = jnp.logical_and(
        owners[:, None] == owners[None, :], tile_iota[None, :] < tile_iota[:, None]
    )
    slots = owners * CAP + jnp.sum(earlier, axis=1).astype(jnp.int32)
    details = jnp.stack([slots, map_slot, starts_here, correlation], axis=0)[None]

    sent = pl.pallas_call(
        filter_kernel,
        out_shape=jax.ShapeDtypeStruct((rows_count * 2 * dates_here, ranges_count), jnp.bfloat16),
        in_specs=[SMEM, VMEM, VMEM],
        out_specs=VMEM,
        scratch_shapes=[pltpu.VMEM((sides, rows_count * 2 * dates_here, TILE), jnp.float32)],
        compiler_params=params,
        name="filter",
    )(filter_lengths, filter_taps, radar_stack)
    sent = sent.reshape(peers, line_count * 2 * dates_here, ranges_count)
    got_lines = lax.all_to_all(sent, "date", split_axis=0, concat_axis=0, tiled=True)
    all_details = lax.all_gather(details, "date", axis=0, tiled=True)

    mixed = dates_here == 8 and peers % 2 == 0
    got_lines = got_lines.reshape(peers, line_count, 2 * dates_here, ranges_count)
    if not mixed:
        got_lines = got_lines.reshape(peers, line_count, 2, dates_here, ranges_count)
        got_lines = got_lines.transpose(1, 2, 0, 3, 4).reshape(1, line_count, 2 * dates, ranges_count)
    packed = pl.pallas_call(
        partial(whiten_kernel, mixed=mixed),
        out_shape=jax.ShapeDtypeStruct((slot_count, 2 * dates, TILE), jnp.bfloat16),
        in_specs=[SMEM, VMEM],
        out_specs=VMEM,
        scratch_shapes=[pltpu.VMEM((window_count, 2 * dates, TILE), jnp.bfloat16)],
        compiler_params=params,
        name="whiten",
    )(slots, got_lines)
    packed = packed.reshape(peers, CAP, 2 * dates, TILE)
    got_tiles = lax.all_to_all(packed, "date", split_axis=0, concat_axis=0, tiled=True)
    got_tiles = got_tiles.reshape(slot_count, 2 * dates, TILE)

    here = me * CAP + jnp.arange(CAP, dtype=jnp.int32)
    match = (all_details[:, None, 0, :] == here[None, :, None]).reshape(slot_count, tile_count)
    fields = jnp.repeat(all_details[:, 1:], CAP, axis=0).reshape(slot_count, 3, tile_count)
    chosen = jnp.sum(jnp.where(match[:, None, :], fields, 0), axis=2)
    filled = jnp.any(match, axis=1)
    weights = chosen[:, 2].astype(jnp.float32)
    map_iota = jnp.arange(MAP_DEV, dtype=jnp.int32)
    on_map = jnp.logical_and(chosen[:, 0][:, None] == map_iota[None, :], filled[:, None])
    sums = jnp.sum(jnp.where(on_map, weights[:, None], 0.0), axis=0)
    scale = jnp.sum(jnp.where(on_map, 1.0 / jnp.maximum(sums, 1.0)[None, :], 0.0), axis=1) * weights
    slot_iota = jnp.arange(slot_count, dtype=jnp.int32)
    place = jnp.sum(jnp.logical_and(filled[None, :], slot_iota[None, :] < slot_iota[:, None]), axis=1)
    count = jnp.sum(filled).astype(jnp.int32)
    taken = jnp.logical_and(place[None, :] == slot_iota[:, None], filled[None, :])

    def listed(values, empty):
        return jnp.where(
            slot_iota < count, jnp.sum(jnp.where(taken, values[None, :], 0), axis=1), empty
        )

    first = jnp.min(jnp.where(filled, slot_iota, slot_count - 1))
    order = listed(slot_iota, first)
    targets = listed(chosen[:, 0], 0)
    begins = listed((TILE - chosen[:, 1]) & (TILE - 1), 0)
    scales = listed(scale, 0.0)
    rounded_kernel = lax.optimization_barrier(resample_kernel.astype(jnp.bfloat16)).astype(jnp.float32)

    return pl.pallas_call(
        map_kernel,
        out_shape=jax.ShapeDtypeStruct((MAP_DEV, 2 * dates, TILE), jnp.float32),
        in_specs=[SMEM, SMEM, SMEM, SMEM, SMEM, SMEM, VMEM],
        out_specs=VMEM,
        scratch_shapes=[pltpu.VMEM((2 * TILE, TILE), jnp.float32)],
        compiler_params=params,
        name="map",
    )(order, targets, begins, count[None], rounded_kernel, scales, got_tiles)


def solution(mesh):
    in_specs = (
        P(None, "date", "grp", None),
        P(None, "date", None),
        P("date"),
        P(),
        P(("grp", "date"), None),
        P(("grp", "date")),
        P(("grp", "date")),
        P(("grp", "date")),
    )
    out_specs = P(("grp", "date"), None, None)
    return jax.shard_map(shards, mesh=mesh, in_specs=in_specs, out_specs=out_specs, check_vma=False)
```

```python
from functools import partial

import jax
import jax.numpy as jnp
from jax import lax
from jax.experimental import pallas as pl
from jax.experimental.pallas import tpu as pltpu
from jax.sharding import PartitionSpec as P

PATCH_AZ = 8
PATCH_RG = 16
TILE = 128
KW = 4
CAP = 2
MAP_DEV = 8
GROUP = 4
PIECES = 4
ARRIVALS = 4

diag_load = 0.5
small_eps = 1e-05
VMEM = pl.BlockSpec(memory_space=pltpu.VMEM)
SMEM = pl.BlockSpec(memory_space=pltpu.SMEM)
HBM = pl.BlockSpec(memory_space=pltpu.HBM)
MIB = 1024 * 1024
params = pltpu.CompilerParams(vmem_limit_bytes=32 * MIB)
wide_params = pltpu.CompilerParams(vmem_limit_bytes=60 * MIB)


def filter_kernel(lengths_hbm, taps_hbm, radar, sent, lengths, taps, columns, staged, rounded, sems, out_sems):
    _, dates_here, rows_count, ranges_count = radar.shape
    tap_count = taps.shape[2]
    period = rows_count + tap_count
    copy_lengths = pltpu.make_async_copy(lengths_hbm, lengths, sems.at[dates_here])
    copy_taps = pltpu.make_async_copy(taps_hbm, taps, sems.at[dates_here + 1])
    copies = [
        pltpu.make_async_copy(radar.at[:, date], columns.at[date], sems.at[date])
        for date in range(dates_here)
    ]
    copy_lengths.start()
    copy_taps.start()
    for copy in copies:
        copy.start()
    copy_lengths.wait()
    copy_taps.wait()
    position = lax.broadcasted_iota(jnp.int32, (1, tap_count), 1)
    for date in range(dates_here):
        mats = []
        for part in range(2):
            used = jnp.where(position < lengths[date], taps[part, pl.ds(date, 1), :], 0.0)
            padded = jnp.concatenate([used, jnp.zeros((1, period - tap_count), jnp.float32)], axis=1)
            spread = jnp.broadcast_to(padded, (rows_count, period))
            rolled = pltpu.roll(spread, period - tap_count // 2, 1, stride=1, stride_axis=0)
            mats.append(rolled[:, :rows_count])
        real_mat, imag_mat = mats
        copies[date].wait()
        cells = columns[date].reshape(2 * rows_count, ranges_count)
        for part, halves in enumerate(((real_mat, -imag_mat), (imag_mat, real_mat))):
            operator = jnp.concatenate(halves, axis=1).astype(jnp.bfloat16)
            product = jnp.dot(operator, cells, preferred_element_type=jnp.float32)
            for side in range(ranges_count // TILE):
                skewed = pltpu.roll(
                    product[:, side * TILE : (side + 1) * TILE], 0, 1, stride=PATCH_RG, stride_axis=0
                )
                first = part * dates_here + date
                staged[side, pl.ds(first, rows_count, stride=2 * dates_here), :] = skewed
    total = sent.shape[0]
    pieces = []
    for piece in range(PIECES):
        rows = pl.ds(piece * (total // PIECES), total // PIECES)
        for side in range(ranges_count // TILE):
            rounded[rows, side * TILE : (side + 1) * TILE] = staged[side, rows, :].astype(jnp.bfloat16)
        pieces.append(pltpu.make_async_copy(rounded.at[rows], sent.at[rows], out_sems.at[piece]))
        pieces[-1].start()
    for piece in pieces:
        piece.wait()


def barrel(blocks, lane_block):
    count = len(blocks)
    step = 1
    while step < count:
        taken = (lane_block & step) != 0
        blocks = [jnp.where(taken, blocks[(i + step) % count], blocks[i]) for i in range(count)]
        step *= 2
    return blocks


def embedded(real_part, imag_part):
    upper = jnp.concatenate([real_part, -imag_part], axis=1)
    lower = jnp.concatenate([imag_part, real_part], axis=1)
    return jnp.concatenate([upper, lower], axis=0)


def whiten_group(cells):
    dates, looks = cells[0].shape[0] // 2, cells[0].shape[1]
    row = lax.broadcasted_iota(jnp.int32, (dates, dates), 0)
    col = lax.broadcasted_iota(jnp.int32, (dates, dates), 1)
    diagonal = row == col
    grams = []
    for cell in cells:
        real_part, imag_part = cell[:dates], cell[dates:]
        straight = jnp.concatenate([real_part, imag_part], axis=1)
        turned = jnp.concatenate([imag_part, -real_part], axis=1)
        left = jnp.concatenate([straight, turned], axis=0)
        grams.append(
            lax.dot_general(left, straight, (((1,), (1,)), ((), ())), preferred_element_type=jnp.float32)
        )
    scaled, bounds = [], []
    for gram in grams:
        gram_re, gram_im = gram[:dates], gram[dates:]
        power = jnp.where(diagonal, gram_re, 0.0)
        row_scale = lax.rsqrt(jnp.sum(power, axis=1, keepdims=True) * (1.0 / looks) + small_eps)
        col_scale = lax.rsqrt(jnp.sum(power, axis=0, keepdims=True) * (1.0 / looks) + small_eps)
        col_scale = col_scale * (1.0 / looks)
        size = (jnp.abs(gram_re) + jnp.abs(gram_im)) * row_scale
        sums = jnp.sum(size, axis=0, keepdims=True) * col_scale + diag_load
        inv_bound = 1.0 / jnp.max(sums, axis=1, keepdims=True)
        factor = row_scale * (col_scale * inv_bound)
        load = jnp.where(diagonal, diag_load * inv_bound, 0.0)
        scaled.append(jnp.concatenate([gram_re * factor + load, gram_im * factor], axis=0))
        bounds.append(inv_bound)
    values = [cell.astype(jnp.float32) for cell in cells]
    rounded = list(cells)
    for sweep in range(2):
        mats = [s.astype(jnp.bfloat16) for s in scaled]
        products = [
            jnp.dot(
                embedded(m[:dates], m[dates:]),
                jnp.concatenate([m, r], axis=1),
                preferred_element_type=jnp.float32,
            )
            for m, r in zip(mats, rounded)
        ]
        scaled = [2.0 * s - p[:, :dates] for s, p in zip(scaled, products)]
        values = [2.0 * v - p[:, dates:] for v, p in zip(values, products)]
        rounded = [v.astype(jnp.bfloat16) for v in values]
    mats = [s.astype(jnp.bfloat16) for s in scaled]
    products = [
        jnp.dot(embedded(m[:dates], m[dates:]), r, preferred_element_type=jnp.float32)
        for m, r in zip(mats, rounded)
    ]
    return [
        ((2.0 * v - p) * b).astype(jnp.bfloat16) for v, p, b in zip(values, products, bounds)
    ]


def whiten_kernel(slots, lines, packed, windows, tiles, sems, *, mixed):
    senders, line_count, part_rows, ranges_count = lines.shape
    dates = windows.shape[1] // 2
    sides = ranges_count // TILE
    lane_block = lax.broadcasted_iota(jnp.int32, (1, TILE), 1) // PATCH_RG
    per_side = TILE // PATCH_RG
    for side in range(sides):
        lanes = pl.ds(side * TILE, TILE)
        if mixed:
            half = part_rows // 2
            for first in range(0, senders, 2):
                blocks = [
                    lines[first : first + 2, a, :, lanes].astype(jnp.float32) for a in range(line_count)
                ]
                found = barrel(blocks, lane_block[:, None])
                rows = pl.ds(first * half, 2 * half)
                rows_im = pl.ds(dates + first * half, 2 * half)
                for w in range(per_side):
                    block = found[-w % per_side]
                    real_part = block[:, :half].reshape(2 * half, TILE)
                    imag_part = block[:, half:].reshape(2 * half, TILE)
                    windows[side * per_side + w, rows, :] = real_part.astype(jnp.bfloat16)
                    windows[side * per_side + w, rows_im, :] = imag_part.astype(jnp.bfloat16)
        else:
            for first in range(0, 2 * dates, 16):
                rows = pl.ds(first, 16)
                blocks = [lines[0, a, rows, lanes].astype(jnp.float32) for a in range(line_count)]
                found = barrel(blocks, lane_block)
                for w in range(per_side):
                    windows[side * per_side + w, rows, :] = found[-w % per_side].astype(jnp.bfloat16)

    def group_step(step, carry):
        first = step * GROUP
        results = whiten_group([windows[first + k] for k in range(GROUP)])
        for k in range(GROUP):
            windows[first + k] = results[k]
        return carry

    lax.fori_loop(0, windows.shape[0] // GROUP, group_step, 0)
    copies = []
    for side in range(sides):
        for first in range(0, 2 * dates, 16):
            rows = pl.ds(first, 16)
            blocks = [
                windows[side * per_side + w, rows, :].astype(jnp.float32) for w in range(per_side)
            ]
            found = barrel(blocks, lane_block)
            for a in range(line_count):
                tiles[a * sides + side, rows, :] = found[-a % per_side].astype(jnp.bfloat16)
        for a in range(line_count):
            at = a * sides + side
            copies.append(pltpu.make_async_copy(tiles.at[at], packed.at[slots[at]], sems.at[at]))
            copies[-1].start()
    for copy in copies:
        copy.wait()


def map_kernel(order, targets, starts, count, kernel, scales, got, out, circulant):
    found = count[0]
    source = lax.broadcasted_iota(jnp.int32, circulant.shape, 0)
    column = lax.broadcasted_iota(jnp.int32, circulant.shape, 1)
    lag = (source - column) & (TILE - 1)
    taps = jnp.zeros(circulant.shape, jnp.float32)
    for k in range(KW):
        taps = jnp.where(lag == k, kernel[k], taps)
    circulant[...] = taps
    out[...] = jnp.zeros(out.shape, jnp.float32)

    def group_step(step, carry):
        first = step * ARRIVALS
        products = []
        for k in range(ARRIVALS):
            at = first + k
            matrix = circulant[pl.ds(starts[at], TILE), :].astype(jnp.bfloat16)
            product = jnp.dot(got[order[at]], matrix, preferred_element_type=jnp.float32)
            products.append(product * scales[at])
        for k in range(ARRIVALS):
            target = targets[first + k]
            out[target] = out[target] + products[k]
        return carry

    lax.fori_loop(0, (found + ARRIVALS - 1) // ARRIVALS, group_step, 0)


def gathered(block, axis_name):
    peers = lax.axis_size(axis_name)
    if peers & (peers - 1):
        return lax.all_gather(block, axis_name, axis=0, tiled=True)
    me = lax.axis_index(axis_name)
    step = 1
    while step < peers:
        other = lax.ppermute(block, axis_name, [(i, i ^ step) for i in range(peers)])
        lower = (me & step) == 0
        block = jnp.where(
            lower, jnp.concatenate([block, other], axis=0), jnp.concatenate([other, block], axis=0)
        )
        step *= 2
    return block


def shards(
    radar_stack,
    filter_taps,
    filter_lengths,
    resample_kernel,
    tile_owner,
    map_slot,
    correlation,
    offsets,
):
    peers = lax.axis_size("date")
    me = lax.axis_index("date")
    _, dates_here, rows_count, ranges_count = radar_stack.shape
    dates = dates_here * peers
    line_count = rows_count // peers
    sides = ranges_count // TILE
    tile_count = line_count * sides
    slot_count = peers * CAP
    window_count = (line_count // PATCH_AZ) * (ranges_count // PATCH_RG)
    assert line_count == PATCH_AZ

    sent = pl.pallas_call(
        filter_kernel,
        out_shape=pltpu.HBM((rows_count * 2 * dates_here, ranges_count), jnp.bfloat16),
        in_specs=[HBM, HBM, HBM],
        out_specs=HBM,
        scratch_shapes=[
            pltpu.SMEM((dates_here,), jnp.int32),
            pltpu.VMEM(filter_taps.shape, jnp.float32),
            pltpu.VMEM((dates_here, 2, rows_count, ranges_count), jnp.bfloat16),
            pltpu.VMEM((sides, rows_count * 2 * dates_here, TILE), jnp.float32),
            pltpu.VMEM((rows_count * 2 * dates_here, ranges_count), jnp.bfloat16),
            pltpu.SemaphoreType.DMA((dates_here + 2,)),
            pltpu.SemaphoreType.DMA((PIECES,)),
        ],
        compiler_params=wide_params,
        name="filter",
    )(filter_lengths, filter_taps, radar_stack)
    sent, tile_owner, map_slot, correlation, offsets = lax.optimization_barrier(
        (sent, tile_owner, map_slot, correlation, offsets)
    )
    owners = tile_owner[:, 0]
    tile_iota = jnp.arange(tile_count, dtype=jnp.int32)
    starts_here = offsets + PATCH_RG * (tile_iota // sides)
    earlier = jnp.logical_and(
        owners[:, None] == owners[None, :], tile_iota[None, :] < tile_iota[:, None]
    )
    slots = owners * CAP + jnp.sum(earlier, axis=1).astype(jnp.int32)
    details = jnp.stack([slots, map_slot, starts_here, correlation], axis=0)[None]
    sent = sent.reshape(peers, line_count * 2 * dates_here, ranges_count)
    got_lines = lax.all_to_all(sent, "date", split_axis=0, concat_axis=0, tiled=True)
    all_details = gathered(details, "date")

    mixed = dates_here == 8 and peers % 2 == 0
    got_lines = got_lines.reshape(peers, line_count, 2 * dates_here, ranges_count)
    if not mixed:
        got_lines = got_lines.reshape(peers, line_count, 2, dates_here, ranges_count)
        got_lines = got_lines.transpose(1, 2, 0, 3, 4).reshape(1, line_count, 2 * dates, ranges_count)
    packed = pl.pallas_call(
        partial(whiten_kernel, mixed=mixed),
        out_shape=pltpu.HBM((slot_count, 2 * dates, TILE), jnp.bfloat16),
        in_specs=[SMEM, VMEM],
        out_specs=HBM,
        scratch_shapes=[
            pltpu.VMEM((window_count, 2 * dates, TILE), jnp.bfloat16),
            pltpu.VMEM((tile_count, 2 * dates, TILE), jnp.bfloat16),
            pltpu.SemaphoreType.DMA((tile_count,)),
        ],
        compiler_params=params,
        name="whiten",
    )(slots, got_lines)
    packed, all_details = lax.optimization_barrier((packed, all_details))
    packed = packed.reshape(peers, CAP, 2 * dates, TILE)
    got_tiles = lax.all_to_all(packed, "date", split_axis=0, concat_axis=0, tiled=True)
    got_tiles = got_tiles.reshape(slot_count, 2 * dates, TILE)

    here = me * CAP + jnp.arange(CAP, dtype=jnp.int32)
    match = (all_details[:, None, 0, :] == here[None, :, None]).reshape(slot_count, tile_count)
    fields = jnp.repeat(all_details[:, 1:], CAP, axis=0).reshape(slot_count, 3, tile_count)
    chosen = jnp.sum(jnp.where(match[:, None, :], fields, 0), axis=2)
    filled = jnp.any(match, axis=1)
    weights = chosen[:, 2].astype(jnp.float32)
    map_iota = jnp.arange(MAP_DEV, dtype=jnp.int32)
    on_map = jnp.logical_and(chosen[:, 0][:, None] == map_iota[None, :], filled[:, None])
    sums = jnp.sum(jnp.where(on_map, weights[:, None], 0.0), axis=0)
    scale = jnp.sum(jnp.where(on_map, 1.0 / jnp.maximum(sums, 1.0)[None, :], 0.0), axis=1) * weights
    slot_iota = jnp.arange(slot_count, dtype=jnp.int32)
    place = jnp.sum(jnp.logical_and(filled[None, :], slot_iota[None, :] < slot_iota[:, None]), axis=1)
    count = jnp.sum(filled).astype(jnp.int32)
    taken = jnp.logical_and(place[None, :] == slot_iota[:, None], filled[None, :])

    def listed(values, empty):
        return jnp.where(
            slot_iota < count, jnp.sum(jnp.where(taken, values[None, :], 0), axis=1), empty
        )

    first = jnp.min(jnp.where(filled, slot_iota, slot_count - 1))
    order = listed(slot_iota, first)
    targets = listed(chosen[:, 0], 0)
    begins = listed((TILE - chosen[:, 1]) & (TILE - 1), 0)
    scales = listed(scale, 0.0)
    rounded_kernel = lax.optimization_barrier(resample_kernel.astype(jnp.bfloat16)).astype(jnp.float32)

    return pl.pallas_call(
        map_kernel,
        out_shape=jax.ShapeDtypeStruct((MAP_DEV, 2 * dates, TILE), jnp.float32),
        in_specs=[SMEM, SMEM, SMEM, SMEM, SMEM, SMEM, VMEM],
        out_specs=VMEM,
        scratch_shapes=[pltpu.VMEM((2 * TILE, TILE), jnp.float32)],
        compiler_params=params,
        name="map",
    )(order, targets, begins, count[None], rounded_kernel, scales, got_tiles)


def solution(mesh):
    in_specs = (
        P(None, "date", "grp", None),
        P(None, "date", None),
        P("date"),
        P(),
        P(("grp", "date"), None),
        P(("grp", "date")),
        P(("grp", "date")),
        P(("grp", "date")),
    )
    out_specs = P(("grp", "date"), None, None)
    return jax.shard_map(shards, mesh=mesh, in_specs=in_specs, out_specs=out_specs, check_vma=False)
```

```python
from functools import partial

import jax
import jax.numpy as jnp
from jax import lax
from jax.experimental import pallas as pl
from jax.experimental.pallas import tpu as pltpu
from jax.sharding import PartitionSpec as P

PATCH_AZ = 8
PATCH_RG = 16
TILE = 128
KW = 4
CAP = 2
MAP_DEV = 8
GROUP = 8
PIECES = 4
ARRIVALS = 4
HALVES = 1

diag_load = 0.5
small_eps = 1e-05
VMEM = pl.BlockSpec(memory_space=pltpu.VMEM)
SMEM = pl.BlockSpec(memory_space=pltpu.SMEM)
HBM = pl.BlockSpec(memory_space=pltpu.HBM)
MIB = 1024 * 1024
params = pltpu.CompilerParams(vmem_limit_bytes=32 * MIB)
wide_params = pltpu.CompilerParams(vmem_limit_bytes=60 * MIB)


def filter_kernel(lengths_hbm, taps_hbm, radar, sent, lengths, taps, columns, staged, rounded, sems, out_sems):
    _, dates_here, rows_count, ranges_count = radar.shape
    tap_count = taps.shape[2]
    period = rows_count + tap_count
    copy_lengths = pltpu.make_async_copy(lengths_hbm, lengths, sems.at[dates_here])
    copy_taps = pltpu.make_async_copy(taps_hbm, taps, sems.at[dates_here + 1])
    copies = [
        pltpu.make_async_copy(radar.at[:, date], columns.at[date], sems.at[date])
        for date in range(dates_here)
    ]
    copy_lengths.start()
    copy_taps.start()
    for copy in copies:
        copy.start()
    copy_lengths.wait()
    copy_taps.wait()
    position = lax.broadcasted_iota(jnp.int32, (1, tap_count), 1)
    for date in range(dates_here):
        mats = []
        for part in range(2):
            used = jnp.where(position < lengths[date], taps[part, pl.ds(date, 1), :], 0.0)
            padded = jnp.concatenate([used, jnp.zeros((1, period - tap_count), jnp.float32)], axis=1)
            spread = jnp.broadcast_to(padded, (rows_count, period))
            rolled = pltpu.roll(spread, period - tap_count // 2, 1, stride=1, stride_axis=0)
            mats.append(rolled[:, :rows_count])
        real_mat, imag_mat = mats
        copies[date].wait()
        cells = columns[date].reshape(2 * rows_count, ranges_count)
        for part, halves in enumerate(((real_mat, -imag_mat), (imag_mat, real_mat))):
            operator = jnp.concatenate(halves, axis=1).astype(jnp.bfloat16)
            product = jnp.dot(operator, cells, preferred_element_type=jnp.float32)
            for side in range(ranges_count // TILE):
                skewed = pltpu.roll(
                    product[:, side * TILE : (side + 1) * TILE], 0, 1, stride=PATCH_RG, stride_axis=0
                )
                first = part * dates_here + date
                staged[side, pl.ds(first, rows_count, stride=2 * dates_here), :] = skewed
    total = sent.shape[0]
    pieces = []
    for piece in range(PIECES):
        rows = pl.ds(piece * (total // PIECES), total // PIECES)
        for side in range(ranges_count // TILE):
            rounded[rows, side * TILE : (side + 1) * TILE] = staged[side, rows, :].astype(jnp.bfloat16)
        pieces.append(pltpu.make_async_copy(rounded.at[rows], sent.at[rows], out_sems.at[piece]))
        pieces[-1].start()
    for piece in pieces:
        piece.wait()


def barrel(blocks, lane_block):
    count = len(blocks)
    step = 1
    while step < count:
        taken = (lane_block & step) != 0
        blocks = [jnp.where(taken, blocks[(i + step) % count], blocks[i]) for i in range(count)]
        step *= 2
    return blocks


def embedded(real_part, imag_part):
    upper = jnp.concatenate([real_part, -imag_part], axis=1)
    lower = jnp.concatenate([imag_part, real_part], axis=1)
    return jnp.concatenate([upper, lower], axis=0)


def whiten_group(cells):
    dates, looks = cells[0].shape[0] // 2, cells[0].shape[1]
    row = lax.broadcasted_iota(jnp.int32, (dates, dates), 0)
    col = lax.broadcasted_iota(jnp.int32, (dates, dates), 1)
    diagonal = row == col
    grams = []
    for cell in cells:
        real_part, imag_part = cell[:dates], cell[dates:]
        straight = jnp.concatenate([real_part, imag_part], axis=1)
        turned = jnp.concatenate([imag_part, -real_part], axis=1)
        left = jnp.concatenate([straight, turned], axis=0)
        grams.append(
            lax.dot_general(left, straight, (((1,), (1,)), ((), ())), preferred_element_type=jnp.float32)
        )
    scaled, bounds = [], []
    for gram in grams:
        gram_re, gram_im = gram[:dates], gram[dates:]
        power = jnp.where(diagonal, gram_re, 0.0)
        row_scale = lax.rsqrt(jnp.sum(power, axis=1, keepdims=True) * (1.0 / looks) + small_eps)
        col_scale = lax.rsqrt(jnp.sum(power, axis=0, keepdims=True) * (1.0 / looks) + small_eps)
        col_scale = col_scale * (1.0 / looks)
        size = (jnp.abs(gram_re) + jnp.abs(gram_im)) * row_scale
        sums = jnp.sum(size, axis=0, keepdims=True) * col_scale + diag_load
        inv_bound = 1.0 / jnp.max(sums, axis=1, keepdims=True)
        factor = row_scale * (col_scale * inv_bound)
        load = jnp.where(diagonal, diag_load * inv_bound, 0.0)
        scaled.append(jnp.concatenate([gram_re * factor + load, gram_im * factor], axis=0))
        bounds.append(inv_bound)
    values = [cell.astype(jnp.float32) for cell in cells]
    rounded = list(cells)
    for sweep in range(2):
        mats = [s.astype(jnp.bfloat16) for s in scaled]
        products = [
            jnp.dot(
                embedded(m[:dates], m[dates:]),
                jnp.concatenate([m, r], axis=1),
                preferred_element_type=jnp.float32,
            )
            for m, r in zip(mats, rounded)
        ]
        scaled = [2.0 * s - p[:, :dates] for s, p in zip(scaled, products)]
        values = [2.0 * v - p[:, dates:] for v, p in zip(values, products)]
        rounded = [v.astype(jnp.bfloat16) for v in values]
    mats = [s.astype(jnp.bfloat16) for s in scaled]
    products = [
        jnp.dot(embedded(m[:dates], m[dates:]), r, preferred_element_type=jnp.float32)
        for m, r in zip(mats, rounded)
    ]
    return [
        ((2.0 * v - p) * b).astype(jnp.bfloat16) for v, p, b in zip(values, products, bounds)
    ]


def whiten_kernel(slots, crossing, lines, leaving, staying, windows, tiles, sems, *, mixed):
    senders, line_count, part_rows, ranges_count = lines.shape
    dates = windows.shape[1] // 2
    sides = ranges_count // TILE
    lane_block = lax.broadcasted_iota(jnp.int32, (1, TILE), 1) // PATCH_RG
    per_side = TILE // PATCH_RG
    for side in range(sides):
        lanes = pl.ds(side * TILE, TILE)
        if mixed:
            half = part_rows // 2
            for first in range(0, senders, 2):
                blocks = [
                    lines[first : first + 2, a, :, lanes].astype(jnp.float32) for a in range(line_count)
                ]
                found = barrel(blocks, lane_block[:, None])
                rows = pl.ds(first * half, 2 * half)
                rows_im = pl.ds(dates + first * half, 2 * half)
                for w in range(per_side):
                    block = found[-w % per_side]
                    real_part = block[:, :half].reshape(2 * half, TILE)
                    imag_part = block[:, half:].reshape(2 * half, TILE)
                    windows[side * per_side + w, rows, :] = real_part.astype(jnp.bfloat16)
                    windows[side * per_side + w, rows_im, :] = imag_part.astype(jnp.bfloat16)
        else:
            for first in range(0, 2 * dates, 16):
                rows = pl.ds(first, 16)
                blocks = [lines[0, a, rows, lanes].astype(jnp.float32) for a in range(line_count)]
                found = barrel(blocks, lane_block)
                for w in range(per_side):
                    windows[side * per_side + w, rows, :] = found[-w % per_side].astype(jnp.bfloat16)

    def group_step(step, carry):
        first = step * GROUP
        results = whiten_group([windows[first + k] for k in range(GROUP)])
        for k in range(GROUP):
            windows[first + k] = results[k]
        return carry

    lax.fori_loop(0, windows.shape[0] // GROUP, group_step, 0)
    copies = []
    for side in range(sides):
        for first in range(0, 2 * dates, 16):
            rows = pl.ds(first, 16)
            blocks = [
                windows[side * per_side + w, rows, :].astype(jnp.float32) for w in range(per_side)
            ]
            found = barrel(blocks, lane_block)
            for a in range(line_count):
                tiles[a * sides + side, rows, :] = found[-a % per_side].astype(jnp.bfloat16)
        for a in range(line_count):
            at = a * sides + side
            copies.append(pltpu.make_async_copy(tiles.at[at], leaving.at[slots[at]], sems.at[at]))

            @pl.when(crossing[at] != 0)
            def _():
                copies[-1].start()

            @pl.when(crossing[at] == 0)
            def _():
                pltpu.make_async_copy(tiles.at[at], staying.at[slots[at]], sems.at[at]).start()

    for copy in copies:
        copy.wait()


def map_kernel(targets, starts, scales, kernel, got, out, circulant, total, *, first_row):
    slot_count, rows_here = got.shape[0], out.shape[1]
    source = lax.broadcasted_iota(jnp.int32, circulant.shape, 0)
    column = lax.broadcasted_iota(jnp.int32, circulant.shape, 1)
    lag = (source - column) & (TILE - 1)
    taps = jnp.zeros(circulant.shape, jnp.float32)
    for k in range(KW):
        taps = jnp.where(lag == k, kernel[k], taps)
    circulant[...] = taps
    total[...] = jnp.zeros(total.shape, jnp.float32)

    def group_step(step, carry):
        products = []
        for k in range(ARRIVALS):
            at = step * ARRIVALS + k
            matrix = circulant[pl.ds(starts[at], TILE), :].astype(jnp.bfloat16)
            tile = got[at, pl.ds(first_row, rows_here), :]
            tile = jnp.where(scales[at] > 0.0, tile, jnp.zeros_like(tile))
            product = jnp.dot(tile, matrix, preferred_element_type=jnp.float32)
            products.append(product * scales[at])
        for k in range(ARRIVALS):
            target = targets[step * ARRIVALS + k]
            total[target] = total[target] + products[k]
        return carry

    lax.fori_loop(0, slot_count // ARRIVALS, group_step, 0)
    out[...] = total[...].astype(out.dtype)


def gathered(block, axis_name):
    peers = lax.axis_size(axis_name)
    if peers & (peers - 1):
        return lax.all_gather(block, axis_name, axis=0, tiled=True)
    me = lax.axis_index(axis_name)
    step = 1
    while step < peers:
        other = lax.ppermute(block, axis_name, [(i, i ^ step) for i in range(peers)])
        lower = (me & step) == 0
        block = jnp.where(
            lower, jnp.concatenate([block, other], axis=0), jnp.concatenate([other, block], axis=0)
        )
        step *= 2
    return block


def arrivals(owner, details, everything):
    senders, _, tile_count = details.shape
    slot_count = senders * CAP
    here = owner * CAP + jnp.arange(CAP, dtype=jnp.int32)
    match = (details[:, None, 0, :] == here[None, :, None]).reshape(slot_count, 1, tile_count)
    fields = jnp.repeat(details[:, 1:], CAP, axis=0).reshape(slot_count, 3, tile_count)
    chosen = jnp.sum(jnp.where(match, fields, 0), axis=2)
    map_iota = jnp.arange(MAP_DEV, dtype=jnp.int32)
    owned = jnp.where(everything[:, 0] // CAP == owner, everything[:, 3], 0).astype(jnp.float32)
    on_map = everything[:, 1][None] == map_iota[:, None, None]
    sums = jnp.sum(jnp.where(on_map, owned[None], 0.0), axis=(1, 2))
    inverse = 1.0 / jnp.maximum(sums, 1.0)
    picked = chosen[:, 0][:, None] == map_iota[None, :]
    scales = jnp.sum(jnp.where(picked, inverse[None, :], 0.0), axis=1) * chosen[:, 2].astype(jnp.float32)
    return chosen[:, 0], (TILE - chosen[:, 1]) & (TILE - 1), scales


def map_sum(lists, rounded_kernel, tiles, kind, name, first_row, rows_here):
    extent = (MAP_DEV, rows_here, TILE)
    return pl.pallas_call(
        partial(map_kernel, first_row=first_row),
        out_shape=jax.ShapeDtypeStruct(extent, kind),
        in_specs=[SMEM, SMEM, SMEM, SMEM, VMEM],
        out_specs=VMEM,
        scratch_shapes=[pltpu.VMEM((2 * TILE, TILE), jnp.float32), pltpu.VMEM(extent, jnp.float32)],
        compiler_params=params,
        name=name,
    )(*lists, rounded_kernel, tiles)


def shards(
    radar_stack,
    filter_taps,
    filter_lengths,
    resample_kernel,
    tile_owner,
    map_slot,
    correlation,
    offsets,
):
    peers = lax.axis_size("date")
    me = lax.axis_index("date")
    _, dates_here, rows_count, ranges_count = radar_stack.shape
    dates = dates_here * peers
    line_count = rows_count // peers
    sides = ranges_count // TILE
    tile_count = line_count * sides
    slot_count = peers * CAP
    window_count = (line_count // PATCH_AZ) * (ranges_count // PATCH_RG)
    assert line_count == PATCH_AZ

    sent = pl.pallas_call(
        filter_kernel,
        out_shape=pltpu.HBM((rows_count * 2 * dates_here, ranges_count), jnp.bfloat16),
        in_specs=[HBM, HBM, HBM],
        out_specs=HBM,
        scratch_shapes=[
            pltpu.SMEM((dates_here,), jnp.int32),
            pltpu.VMEM(filter_taps.shape, jnp.float32),
            pltpu.VMEM((dates_here, 2, rows_count, ranges_count), jnp.bfloat16),
            pltpu.VMEM((sides, rows_count * 2 * dates_here, TILE), jnp.float32),
            pltpu.VMEM((rows_count * 2 * dates_here, ranges_count), jnp.bfloat16),
            pltpu.SemaphoreType.DMA((dates_here + 2,)),
            pltpu.SemaphoreType.DMA((PIECES,)),
        ],
        compiler_params=wide_params,
        name="filter",
    )(filter_lengths, filter_taps, radar_stack)
    sent, tile_owner, map_slot, correlation, offsets = lax.optimization_barrier(
        (sent, tile_owner, map_slot, correlation, offsets)
    )
    owners = tile_owner[:, 0]
    tile_iota = jnp.arange(tile_count, dtype=jnp.int32)
    starts_here = offsets + PATCH_RG * (tile_iota // sides)
    earlier = jnp.logical_and(
        owners[:, None] == owners[None, :], tile_iota[None, :] < tile_iota[:, None]
    )
    half = peers // 2
    ranks = jnp.sum(earlier, axis=1).astype(jnp.int32)
    slots = (owners % half) * CAP + ranks
    crossing = (owners // half != me // half).astype(jnp.int32)
    details = jnp.stack([owners * CAP + ranks, map_slot, starts_here, correlation], axis=0)[None]
    sent = sent.reshape(peers, line_count * 2 * dates_here, ranges_count)
    got_lines = lax.all_to_all(sent, "date", split_axis=0, concat_axis=0, tiled=True)
    all_details = gathered(details, "date")

    mixed = dates_here == 8 and peers % 2 == 0
    got_lines = got_lines.reshape(peers, line_count, 2 * dates_here, ranges_count)
    if not mixed:
        got_lines = got_lines.reshape(peers, line_count, 2, dates_here, ranges_count)
        got_lines = got_lines.transpose(1, 2, 0, 3, 4).reshape(1, line_count, 2 * dates, ranges_count)
    slot_count = half * CAP
    buffer = pltpu.HBM((slot_count, 2 * dates, TILE), jnp.bfloat16)
    leaving, staying = pl.pallas_call(
        partial(whiten_kernel, mixed=mixed),
        out_shape=(buffer, buffer),
        in_specs=[SMEM, SMEM, VMEM],
        out_specs=(HBM, HBM),
        scratch_shapes=[
            pltpu.VMEM((window_count, 2 * dates, TILE), jnp.bfloat16),
            pltpu.VMEM((tile_count, 2 * dates, TILE), jnp.bfloat16),
            pltpu.SemaphoreType.DMA((tile_count,)),
        ],
        compiler_params=params,
        name="whiten",
    )(slots, crossing, got_lines)
    leaving, all_details, resample_kernel = lax.optimization_barrier(
        (leaving, all_details, resample_kernel)
    )
    halves = [list(range(half)), list(range(half, peers))]

    def within_half(tiles):
        return lax.all_to_all(
            tiles, "date", split_axis=0, concat_axis=0, axis_index_groups=halves, tiled=True
        )

    rounded_kernel = lax.optimization_barrier(resample_kernel.astype(jnp.bfloat16)).astype(jnp.float32)
    near = lax.dynamic_slice_in_dim(all_details, me // half * half, half, axis=0)
    gathered_here = within_half(leaving)
    far_lists = arrivals((me + half) % peers, near, all_details)
    near_lists = arrivals(me, near, all_details)
    gathered_here, staying, far_lists, near_lists, rounded_kernel = lax.optimization_barrier(
        (gathered_here, staying, far_lists, near_lists, rounded_kernel)
    )
    across = [(i, (i + half) % peers) for i in range(peers)]
    rows_each = 2 * dates // HALVES
    from_far = []
    for piece in range(HALVES):
        partial_sums = map_sum(
            far_lists, rounded_kernel, gathered_here, jnp.bfloat16, "far_sum", piece * rows_each, rows_each
        )
        if piece + 1 < HALVES:
            partial_sums, gathered_here = lax.optimization_barrier((partial_sums, gathered_here))
        from_far.append(lax.ppermute(partial_sums, "date", across))
    own_sums = map_sum(
        near_lists, rounded_kernel, within_half(staying), jnp.float32, "near_sum", 0, 2 * dates
    )
    return own_sums + jnp.concatenate(from_far, axis=1).astype(jnp.float32)


def solution(mesh):
    in_specs = (
        P(None, "date", "grp", None),
        P(None, "date", None),
        P("date"),
        P(),
        P(("grp", "date"), None),
        P(("grp", "date")),
        P(("grp", "date")),
        P(("grp", "date")),
    )
    out_specs = P(("grp", "date"), None, None)
    return jax.shard_map(shards, mesh=mesh, in_specs=in_specs, out_specs=out_specs, check_vma=False)
```

```python
from functools import partial

import jax
import jax.numpy as jnp
from jax import lax
from jax.experimental import pallas as pl
from jax.experimental.pallas import tpu as pltpu
from jax.sharding import PartitionSpec as P

PATCH_AZ = 8
PATCH_RG = 16
TILE = 128
KW = 4
CAP = 2
MAP_DEV = 8
GROUP = 16
PIECES = 4
ARRIVALS = 8
HALVES = 1

diag_load = 0.5
small_eps = 1e-05
VMEM = pl.BlockSpec(memory_space=pltpu.VMEM)
SMEM = pl.BlockSpec(memory_space=pltpu.SMEM)
HBM = pl.BlockSpec(memory_space=pltpu.HBM)
MIB = 1024 * 1024
params = pltpu.CompilerParams(vmem_limit_bytes=32 * MIB)
wide_params = pltpu.CompilerParams(vmem_limit_bytes=60 * MIB)


def filter_kernel(lengths_hbm, taps_hbm, radar, sent, lengths, taps, columns, staged, rounded, sems, out_sems):
    _, dates_here, rows_count, ranges_count = radar.shape
    tap_count = taps.shape[2]
    period = rows_count + tap_count
    copy_lengths = pltpu.make_async_copy(lengths_hbm, lengths, sems.at[dates_here])
    copy_taps = pltpu.make_async_copy(taps_hbm, taps, sems.at[dates_here + 1])
    copies = [
        pltpu.make_async_copy(radar.at[:, date], columns.at[date], sems.at[date])
        for date in range(dates_here)
    ]
    copy_lengths.start()
    copy_taps.start()
    for copy in copies:
        copy.start()
    copy_lengths.wait()
    copy_taps.wait()
    position = lax.broadcasted_iota(jnp.int32, (1, tap_count), 1)
    operators = []
    for date in range(dates_here):
        mats = []
        for part in range(2):
            used = jnp.where(position < lengths[date], taps[part, pl.ds(date, 1), :], 0.0)
            padded = jnp.concatenate([used, jnp.zeros((1, period - tap_count), jnp.float32)], axis=1)
            spread = jnp.broadcast_to(padded, (rows_count, period))
            rolled = pltpu.roll(spread, period - tap_count // 2, 1, stride=1, stride_axis=0)
            mats.append(rolled[:, :rows_count].astype(jnp.bfloat16))
        operators.append(mats)
    for copy in copies:
        copy.wait()
    for date, (real_mat, imag_mat) in enumerate(operators):
        cells = columns[date].reshape(2 * rows_count, ranges_count)
        for part, halves in enumerate(((real_mat, -imag_mat), (imag_mat, real_mat))):
            operator = jnp.concatenate(halves, axis=1)
            product = jnp.dot(operator, cells, preferred_element_type=jnp.float32)
            for side in range(ranges_count // TILE):
                skewed = pltpu.roll(
                    product[:, side * TILE : (side + 1) * TILE], 0, 1, stride=PATCH_RG, stride_axis=0
                )
                first = part * dates_here + date
                staged[side, pl.ds(first, rows_count, stride=2 * dates_here), :] = skewed
    total = sent.shape[0]
    pieces = []
    for piece in range(PIECES):
        rows = pl.ds(piece * (total // PIECES), total // PIECES)
        for side in range(ranges_count // TILE):
            rounded[rows, side * TILE : (side + 1) * TILE] = staged[side, rows, :].astype(jnp.bfloat16)
        pieces.append(pltpu.make_async_copy(rounded.at[rows], sent.at[rows], out_sems.at[piece]))
        pieces[-1].start()
    for piece in pieces:
        piece.wait()


def barrel(blocks, lane_block):
    count = len(blocks)
    step = 1
    while step < count:
        taken = (lane_block & step) != 0
        blocks = [jnp.where(taken, blocks[(i + step) % count], blocks[i]) for i in range(count)]
        step *= 2
    return blocks


def embedded(real_part, imag_part):
    upper = jnp.concatenate([real_part, -imag_part], axis=1)
    lower = jnp.concatenate([imag_part, real_part], axis=1)
    return jnp.concatenate([upper, lower], axis=0)


def whiten_group(cells):
    dates, looks = cells[0].shape[0] // 2, cells[0].shape[1]
    row = lax.broadcasted_iota(jnp.int32, (dates, dates), 0)
    col = lax.broadcasted_iota(jnp.int32, (dates, dates), 1)
    diagonal = row == col
    grams = []
    for cell in cells:
        real_part, imag_part = cell[:dates], cell[dates:]
        straight = jnp.concatenate([real_part, imag_part], axis=1)
        turned = jnp.concatenate([imag_part, -real_part], axis=1)
        left = jnp.concatenate([straight, turned], axis=0)
        grams.append(
            lax.dot_general(left, straight, (((1,), (1,)), ((), ())), preferred_element_type=jnp.float32)
        )
    scaled, bounds = [], []
    for gram in grams:
        gram_re, gram_im = gram[:dates], gram[dates:]
        power = jnp.where(diagonal, gram_re, 0.0)
        row_scale = lax.rsqrt(jnp.sum(power, axis=1, keepdims=True) * (1.0 / looks) + small_eps)
        col_scale = lax.rsqrt(jnp.sum(power, axis=0, keepdims=True) * (1.0 / looks) + small_eps)
        col_scale = col_scale * (1.0 / looks)
        size = (jnp.abs(gram_re) + jnp.abs(gram_im)) * row_scale
        sums = jnp.sum(size, axis=0, keepdims=True) * col_scale + diag_load
        inv_bound = 1.0 / jnp.max(sums, axis=1, keepdims=True)
        factor = row_scale * (col_scale * inv_bound)
        load = jnp.where(diagonal, diag_load * inv_bound, 0.0)
        scaled.append(jnp.concatenate([gram_re * factor + load, gram_im * factor], axis=0))
        bounds.append(inv_bound)
    values = [cell.astype(jnp.float32) for cell in cells]
    rounded = list(cells)
    for sweep in range(2):
        mats = [s.astype(jnp.bfloat16) for s in scaled]
        products = [
            jnp.dot(
                embedded(m[:dates], m[dates:]),
                jnp.concatenate([m, r], axis=1),
                preferred_element_type=jnp.float32,
            )
            for m, r in zip(mats, rounded)
        ]
        scaled = [2.0 * s - p[:, :dates] for s, p in zip(scaled, products)]
        values = [2.0 * v - p[:, dates:] for v, p in zip(values, products)]
        rounded = [v.astype(jnp.bfloat16) for v in values]
    mats = [s.astype(jnp.bfloat16) for s in scaled]
    products = [
        jnp.dot(embedded(m[:dates], m[dates:]), r, preferred_element_type=jnp.float32)
        for m, r in zip(mats, rounded)
    ]
    return [
        ((2.0 * v - p) * b).astype(jnp.bfloat16) for v, p, b in zip(values, products, bounds)
    ]


def whiten_kernel(slots, crossing, lines, leaving, staying, windows, tiles, sems, *, mixed):
    senders, line_count, part_rows, ranges_count = lines.shape
    dates = windows.shape[1] // 2
    sides = ranges_count // TILE
    lane_block = lax.broadcasted_iota(jnp.int32, (1, TILE), 1) // PATCH_RG
    per_side = TILE // PATCH_RG
    for side in range(sides):
        lanes = pl.ds(side * TILE, TILE)
        if mixed:
            half = part_rows // 2
            for first in range(0, senders, 2):
                blocks = [
                    lines[first : first + 2, a, :, lanes].astype(jnp.float32) for a in range(line_count)
                ]
                found = barrel(blocks, lane_block[:, None])
                rows = pl.ds(first * half, 2 * half)
                rows_im = pl.ds(dates + first * half, 2 * half)
                for w in range(per_side):
                    block = found[-w % per_side]
                    real_part = block[:, :half].reshape(2 * half, TILE)
                    imag_part = block[:, half:].reshape(2 * half, TILE)
                    windows[side * per_side + w, rows, :] = real_part.astype(jnp.bfloat16)
                    windows[side * per_side + w, rows_im, :] = imag_part.astype(jnp.bfloat16)
        else:
            for first in range(0, 2 * dates, 16):
                rows = pl.ds(first, 16)
                blocks = [lines[0, a, rows, lanes].astype(jnp.float32) for a in range(line_count)]
                found = barrel(blocks, lane_block)
                for w in range(per_side):
                    windows[side * per_side + w, rows, :] = found[-w % per_side].astype(jnp.bfloat16)

    def group_step(step, carry):
        first = step * GROUP
        results = whiten_group([windows[first + k] for k in range(GROUP)])
        for k in range(GROUP):
            windows[first + k] = results[k]
        return carry

    lax.fori_loop(0, windows.shape[0] // GROUP, group_step, 0)
    copies = []
    for side in range(sides):
        for first in range(0, 2 * dates, 16):
            rows = pl.ds(first, 16)
            blocks = [
                windows[side * per_side + w, rows, :].astype(jnp.float32) for w in range(per_side)
            ]
            found = barrel(blocks, lane_block)
            for a in range(line_count):
                tiles[a * sides + side, rows, :] = found[-a % per_side].astype(jnp.bfloat16)
        for a in range(line_count):
            at = a * sides + side
            copies.append(pltpu.make_async_copy(tiles.at[at], leaving.at[slots[at]], sems.at[at]))

            @pl.when(crossing[at] != 0)
            def _():
                copies[-1].start()

            @pl.when(crossing[at] == 0)
            def _():
                pltpu.make_async_copy(tiles.at[at], staying.at[slots[at]], sems.at[at]).start()

    for copy in copies:
        copy.wait()


def map_kernel(targets, starts, scales, kernel, got, out, circulant, total, *, first_row):
    slot_count, rows_here = got.shape[0], out.shape[1]
    source = lax.broadcasted_iota(jnp.int32, circulant.shape, 0)
    column = lax.broadcasted_iota(jnp.int32, circulant.shape, 1)
    lag = (source - column) & (TILE - 1)
    taps = jnp.zeros(circulant.shape, jnp.float32)
    for k in range(KW):
        taps = jnp.where(lag == k, kernel[k], taps)
    circulant[...] = taps
    total[...] = jnp.zeros(total.shape, jnp.float32)

    def group_step(step, carry):
        products = []
        for k in range(ARRIVALS):
            at = step * ARRIVALS + k
            matrix = circulant[pl.ds(starts[at], TILE), :].astype(jnp.bfloat16)
            tile = got[at, pl.ds(first_row, rows_here), :]
            tile = jnp.where(scales[at] > 0.0, tile, jnp.zeros_like(tile))
            product = jnp.dot(tile, matrix, preferred_element_type=jnp.float32)
            products.append(product * scales[at])
        for k in range(ARRIVALS):
            target = targets[step * ARRIVALS + k]
            total[target] = total[target] + products[k]
        return carry

    lax.fori_loop(0, slot_count // ARRIVALS, group_step, 0)
    out[...] = total[...].astype(out.dtype)


def gathered(block, axis_name):
    peers = lax.axis_size(axis_name)
    if peers & (peers - 1):
        return lax.all_gather(block, axis_name, axis=0, tiled=True)
    me = lax.axis_index(axis_name)
    step = 1
    while step < peers:
        other = lax.ppermute(block, axis_name, [(i, i ^ step) for i in range(peers)])
        lower = (me & step) == 0
        block = jnp.where(
            lower, jnp.concatenate([block, other], axis=0), jnp.concatenate([other, block], axis=0)
        )
        step *= 2
    return block


def arrivals(owner, details, everything):
    senders, _, tile_count = details.shape
    slot_count = senders * CAP
    here = owner * CAP + jnp.arange(CAP, dtype=jnp.int32)
    match = (details[:, None, 0, :] == here[None, :, None]).reshape(slot_count, 1, tile_count)
    fields = jnp.repeat(details[:, 1:], CAP, axis=0).reshape(slot_count, 3, tile_count)
    chosen = jnp.sum(jnp.where(match, fields, 0), axis=2)
    map_iota = jnp.arange(MAP_DEV, dtype=jnp.int32)
    owned = jnp.where(everything[:, 0] // CAP == owner, everything[:, 3], 0).astype(jnp.float32)
    on_map = everything[:, 1][None] == map_iota[:, None, None]
    sums = jnp.sum(jnp.where(on_map, owned[None], 0.0), axis=(1, 2))
    inverse = 1.0 / jnp.maximum(sums, 1.0)
    picked = chosen[:, 0][:, None] == map_iota[None, :]
    scales = jnp.sum(jnp.where(picked, inverse[None, :], 0.0), axis=1) * chosen[:, 2].astype(jnp.float32)
    return chosen[:, 0], (TILE - chosen[:, 1]) & (TILE - 1), scales


def map_sum(lists, rounded_kernel, tiles, kind, name, first_row, rows_here):
    extent = (MAP_DEV, rows_here, TILE)
    return pl.pallas_call(
        partial(map_kernel, first_row=first_row),
        out_shape=jax.ShapeDtypeStruct(extent, kind),
        in_specs=[SMEM, SMEM, SMEM, SMEM, VMEM],
        out_specs=VMEM,
        scratch_shapes=[pltpu.VMEM((2 * TILE, TILE), jnp.float32), pltpu.VMEM(extent, jnp.float32)],
        compiler_params=params,
        name=name,
    )(*lists, rounded_kernel, tiles)


def shards(
    radar_stack,
    filter_taps,
    filter_lengths,
    resample_kernel,
    tile_owner,
    map_slot,
    correlation,
    offsets,
):
    peers = lax.axis_size("date")
    me = lax.axis_index("date")
    _, dates_here, rows_count, ranges_count = radar_stack.shape
    dates = dates_here * peers
    line_count = rows_count // peers
    sides = ranges_count // TILE
    tile_count = line_count * sides
    slot_count = peers * CAP
    window_count = (line_count // PATCH_AZ) * (ranges_count // PATCH_RG)
    assert line_count == PATCH_AZ

    sent = pl.pallas_call(
        filter_kernel,
        out_shape=pltpu.HBM((rows_count * 2 * dates_here, ranges_count), jnp.bfloat16),
        in_specs=[HBM, HBM, HBM],
        out_specs=HBM,
        scratch_shapes=[
            pltpu.SMEM((dates_here,), jnp.int32),
            pltpu.VMEM(filter_taps.shape, jnp.float32),
            pltpu.VMEM((dates_here, 2, rows_count, ranges_count), jnp.bfloat16),
            pltpu.VMEM((sides, rows_count * 2 * dates_here, TILE), jnp.float32),
            pltpu.VMEM((rows_count * 2 * dates_here, ranges_count), jnp.bfloat16),
            pltpu.SemaphoreType.DMA((dates_here + 2,)),
            pltpu.SemaphoreType.DMA((PIECES,)),
        ],
        compiler_params=wide_params,
        name="filter",
    )(filter_lengths, filter_taps, radar_stack)
    sent, tile_owner, map_slot, correlation, offsets = lax.optimization_barrier(
        (sent, tile_owner, map_slot, correlation, offsets)
    )
    owners = tile_owner[:, 0]
    tile_iota = jnp.arange(tile_count, dtype=jnp.int32)
    starts_here = offsets + PATCH_RG * (tile_iota // sides)
    earlier = jnp.logical_and(
        owners[:, None] == owners[None, :], tile_iota[None, :] < tile_iota[:, None]
    )
    half = peers // 2
    ranks = jnp.sum(earlier, axis=1).astype(jnp.int32)
    slots = (owners % half) * CAP + ranks
    crossing = (owners // half != me // half).astype(jnp.int32)
    details = jnp.stack([owners * CAP + ranks, map_slot, starts_here, correlation], axis=0)[None]
    sent = sent.reshape(peers, line_count * 2 * dates_here, ranges_count)
    got_lines = lax.all_to_all(sent, "date", split_axis=0, concat_axis=0, tiled=True)
    all_details = gathered(details, "date")

    mixed = dates_here == 8 and peers % 2 == 0
    got_lines = got_lines.reshape(peers, line_count, 2 * dates_here, ranges_count)
    if not mixed:
        got_lines = got_lines.reshape(peers, line_count, 2, dates_here, ranges_count)
        got_lines = got_lines.transpose(1, 2, 0, 3, 4).reshape(1, line_count, 2 * dates, ranges_count)
    slot_count = half * CAP
    buffer = pltpu.HBM((slot_count, 2 * dates, TILE), jnp.bfloat16)
    leaving, staying = pl.pallas_call(
        partial(whiten_kernel, mixed=mixed),
        out_shape=(buffer, buffer),
        in_specs=[SMEM, SMEM, VMEM],
        out_specs=(HBM, HBM),
        scratch_shapes=[
            pltpu.VMEM((window_count, 2 * dates, TILE), jnp.bfloat16),
            pltpu.VMEM((tile_count, 2 * dates, TILE), jnp.bfloat16),
            pltpu.SemaphoreType.DMA((tile_count,)),
        ],
        compiler_params=params,
        name="whiten",
    )(slots, crossing, got_lines)
    leaving, all_details, resample_kernel = lax.optimization_barrier(
        (leaving, all_details, resample_kernel)
    )
    halves = [list(range(half)), list(range(half, peers))]

    def within_half(tiles):
        return lax.all_to_all(
            tiles, "date", split_axis=0, concat_axis=0, axis_index_groups=halves, tiled=True
        )

    rounded_kernel = lax.optimization_barrier(resample_kernel.astype(jnp.bfloat16)).astype(jnp.float32)
    near = lax.dynamic_slice_in_dim(all_details, me // half * half, half, axis=0)
    gathered_here = within_half(leaving)
    far_lists = arrivals((me + half) % peers, near, all_details)
    near_lists = arrivals(me, near, all_details)
    gathered_here, staying, far_lists, near_lists, rounded_kernel = lax.optimization_barrier(
        (gathered_here, staying, far_lists, near_lists, rounded_kernel)
    )
    across = [(i, (i + half) % peers) for i in range(peers)]
    rows_each = 2 * dates // HALVES
    from_far = []
    for piece in range(HALVES):
        partial_sums = map_sum(
            far_lists, rounded_kernel, gathered_here, jnp.bfloat16, "far_sum", piece * rows_each, rows_each
        )
        if piece + 1 < HALVES:
            partial_sums, gathered_here = lax.optimization_barrier((partial_sums, gathered_here))
        from_far.append(lax.ppermute(partial_sums, "date", across))
    own_sums = map_sum(
        near_lists, rounded_kernel, within_half(staying), jnp.float32, "near_sum", 0, 2 * dates
    )
    return own_sums + jnp.concatenate(from_far, axis=1).astype(jnp.float32)


def solution(mesh):
    in_specs = (
        P(None, "date", "grp", None),
        P(None, "date", None),
        P("date"),
        P(),
        P(("grp", "date"), None),
        P(("grp", "date")),
        P(("grp", "date")),
        P(("grp", "date")),
    )
    out_specs = P(("grp", "date"), None, None)
    return jax.shard_map(shards, mesh=mesh, in_specs=in_specs, out_specs=out_specs, check_vma=False)
```

```python
from functools import partial

import jax
import jax.numpy as jnp
from jax import lax
from jax.experimental import pallas as pl
from jax.experimental.pallas import tpu as pltpu
from jax.sharding import PartitionSpec as P

PATCH_AZ = 8
PATCH_RG = 16
TILE = 128
KW = 4
CAP = 2
MAP_DEV = 8
GROUP = 16
PIECES = 4
ARRIVALS = 8
HALVES = 1

diag_load = 0.5
small_eps = 1e-05
VMEM = pl.BlockSpec(memory_space=pltpu.VMEM)
SMEM = pl.BlockSpec(memory_space=pltpu.SMEM)
HBM = pl.BlockSpec(memory_space=pltpu.HBM)
MIB = 1024 * 1024
params = pltpu.CompilerParams(vmem_limit_bytes=32 * MIB)
wide_params = pltpu.CompilerParams(vmem_limit_bytes=60 * MIB)


def filter_kernel(lengths_hbm, taps_hbm, radar, sent, lengths, taps, columns, staged, rounded, sems, out_sems):
    _, dates_here, rows_count, ranges_count = radar.shape
    tap_count = taps.shape[2]
    period = rows_count + tap_count
    copy_lengths = pltpu.make_async_copy(lengths_hbm, lengths, sems.at[dates_here])
    copy_taps = pltpu.make_async_copy(taps_hbm, taps, sems.at[dates_here + 1])
    copies = [
        pltpu.make_async_copy(radar.at[:, date], columns.at[date], sems.at[date])
        for date in range(dates_here)
    ]
    copy_lengths.start()
    copy_taps.start()
    for copy in copies:
        copy.start()
    copy_lengths.wait()
    copy_taps.wait()
    position = lax.broadcasted_iota(jnp.int32, (1, tap_count), 1)
    operators = []
    for date in range(dates_here):
        mats = []
        for part in range(2):
            used = jnp.where(position < lengths[date], taps[part, pl.ds(date, 1), :], 0.0)
            padded = jnp.concatenate([used, jnp.zeros((1, period - tap_count), jnp.float32)], axis=1)
            spread = jnp.broadcast_to(padded, (rows_count, period))
            rolled = pltpu.roll(spread, period - tap_count // 2, 1, stride=1, stride_axis=0)
            mats.append(rolled[:, :rows_count].astype(jnp.bfloat16))
        operators.append(mats)
    for copy in copies:
        copy.wait()
    for date, (real_mat, imag_mat) in enumerate(operators):
        cells = columns[date].reshape(2 * rows_count, ranges_count)
        for part, halves in enumerate(((real_mat, -imag_mat), (imag_mat, real_mat))):
            operator = jnp.concatenate(halves, axis=1)
            product = jnp.dot(operator, cells, preferred_element_type=jnp.float32)
            for side in range(ranges_count // TILE):
                skewed = pltpu.roll(
                    product[:, side * TILE : (side + 1) * TILE], 0, 1, stride=PATCH_RG, stride_axis=0
                )
                first = part * dates_here + date
                staged[side, pl.ds(first, rows_count, stride=2 * dates_here), :] = skewed
    total = sent.shape[0]
    pieces = []
    for piece in range(PIECES):
        rows = pl.ds(piece * (total // PIECES), total // PIECES)
        for side in range(ranges_count // TILE):
            rounded[rows, side * TILE : (side + 1) * TILE] = staged[side, rows, :].astype(jnp.bfloat16)
        pieces.append(pltpu.make_async_copy(rounded.at[rows], sent.at[rows], out_sems.at[piece]))
        pieces[-1].start()
    for piece in pieces:
        piece.wait()


def barrel(blocks, lane_block):
    count = len(blocks)
    step = 1
    while step < count:
        taken = (lane_block & step) != 0
        blocks = [jnp.where(taken, blocks[(i + step) % count], blocks[i]) for i in range(count)]
        step *= 2
    return blocks


def embedded(real_part, imag_part):
    upper = jnp.concatenate([real_part, -imag_part], axis=1)
    lower = jnp.concatenate([imag_part, real_part], axis=1)
    return jnp.concatenate([upper, lower], axis=0)


def whiten_group(cells):
    dates, looks = cells[0].shape[0] // 2, cells[0].shape[1]
    row = lax.broadcasted_iota(jnp.int32, (dates, dates), 0)
    col = lax.broadcasted_iota(jnp.int32, (dates, dates), 1)
    diagonal = row == col
    grams = []
    for cell in cells:
        real_part, imag_part = cell[:dates], cell[dates:]
        straight = jnp.concatenate([real_part, imag_part], axis=1)
        turned = jnp.concatenate([imag_part, -real_part], axis=1)
        left = jnp.concatenate([straight, turned], axis=0)
        grams.append(
            lax.dot_general(left, straight, (((1,), (1,)), ((), ())), preferred_element_type=jnp.float32)
        )
    scaled, bounds = [], []
    for gram in grams:
        gram_re, gram_im = gram[:dates], gram[dates:]
        power = jnp.where(diagonal, gram_re, 0.0)
        row_scale = lax.rsqrt(jnp.sum(power, axis=1, keepdims=True) * (1.0 / looks) + small_eps)
        col_scale = lax.rsqrt(jnp.sum(power, axis=0, keepdims=True) * (1.0 / looks) + small_eps)
        col_scale = col_scale * (1.0 / looks)
        size = (jnp.abs(gram_re) + jnp.abs(gram_im)) * row_scale
        sums = jnp.sum(size, axis=0, keepdims=True) * col_scale + diag_load
        inv_bound = 1.0 / jnp.max(sums, axis=1, keepdims=True)
        factor = row_scale * (col_scale * inv_bound)
        load = jnp.where(diagonal, diag_load * inv_bound, 0.0)
        scaled.append(jnp.concatenate([gram_re * factor + load, gram_im * factor], axis=0))
        bounds.append(inv_bound)
    values = [cell.astype(jnp.float32) for cell in cells]
    rounded = list(cells)
    for sweep in range(2):
        mats = [s.astype(jnp.bfloat16) for s in scaled]
        products = [
            jnp.dot(
                embedded(m[:dates], m[dates:]),
                jnp.concatenate([m, r], axis=1),
                preferred_element_type=jnp.float32,
            )
            for m, r in zip(mats, rounded)
        ]
        scaled = [2.0 * s - p[:, :dates] for s, p in zip(scaled, products)]
        values = [2.0 * v - p[:, dates:] for v, p in zip(values, products)]
        rounded = [v.astype(jnp.bfloat16) for v in values]
    mats = [s.astype(jnp.bfloat16) for s in scaled]
    products = [
        jnp.dot(embedded(m[:dates], m[dates:]), r, preferred_element_type=jnp.float32)
        for m, r in zip(mats, rounded)
    ]
    return [
        ((2.0 * v - p) * b).astype(jnp.bfloat16) for v, p, b in zip(values, products, bounds)
    ]


def whiten_kernel(slots, routes, lines, leaving, same, other, windows, tiles, sems, *, mixed):
    senders, line_count, part_rows, ranges_count = lines.shape
    dates = windows.shape[1] // 2
    sides = ranges_count // TILE
    lane_block = lax.broadcasted_iota(jnp.int32, (1, TILE), 1) // PATCH_RG
    per_side = TILE // PATCH_RG
    for side in range(sides):
        lanes = pl.ds(side * TILE, TILE)
        if mixed:
            half = part_rows // 2
            for first in range(0, senders, 2):
                blocks = [
                    lines[first : first + 2, a, :, lanes].astype(jnp.float32) for a in range(line_count)
                ]
                found = barrel(blocks, lane_block[:, None])
                rows = pl.ds(first * half, 2 * half)
                rows_im = pl.ds(dates + first * half, 2 * half)
                for w in range(per_side):
                    block = found[-w % per_side]
                    real_part = block[:, :half].reshape(2 * half, TILE)
                    imag_part = block[:, half:].reshape(2 * half, TILE)
                    windows[side * per_side + w, rows, :] = real_part.astype(jnp.bfloat16)
                    windows[side * per_side + w, rows_im, :] = imag_part.astype(jnp.bfloat16)
        else:
            for first in range(0, 2 * dates, 16):
                rows = pl.ds(first, 16)
                blocks = [lines[0, a, rows, lanes].astype(jnp.float32) for a in range(line_count)]
                found = barrel(blocks, lane_block)
                for w in range(per_side):
                    windows[side * per_side + w, rows, :] = found[-w % per_side].astype(jnp.bfloat16)

    def group_step(step, carry):
        first = step * GROUP
        results = whiten_group([windows[first + k] for k in range(GROUP)])
        for k in range(GROUP):
            windows[first + k] = results[k]
        return carry

    lax.fori_loop(0, windows.shape[0] // GROUP, group_step, 0)
    copies = []
    for side in range(sides):
        for first in range(0, 2 * dates, 16):
            rows = pl.ds(first, 16)
            blocks = [
                windows[side * per_side + w, rows, :].astype(jnp.float32) for w in range(per_side)
            ]
            found = barrel(blocks, lane_block)
            for a in range(line_count):
                tiles[a * sides + side, rows, :] = found[-a % per_side].astype(jnp.bfloat16)
        for a in range(line_count):
            at = a * sides + side
            routed = [
                pltpu.make_async_copy(tiles.at[at], buffer.at[slots[at]], sems.at[at])
                for buffer in (leaving, same, other)
            ]
            for route, copy in enumerate(routed):
                pl.when(routes[at] == route)(copy.start)
            copies.append(routed[0])
    for copy in copies:
        copy.wait()


def map_kernel(targets, starts, scales, kernel, *refs, first_row):
    *arrived, out, circulant, total = refs
    rows_here = out.shape[1]
    source = lax.broadcasted_iota(jnp.int32, circulant.shape, 0)
    column = lax.broadcasted_iota(jnp.int32, circulant.shape, 1)
    lag = (source - column) & (TILE - 1)
    taps = jnp.zeros(circulant.shape, jnp.float32)
    for k in range(KW):
        taps = jnp.where(lag == k, kernel[k], taps)
    circulant[...] = taps
    total[...] = jnp.zeros(total.shape, jnp.float32)

    def group_step(got, before, each, step, carry):
        products = []
        for k in range(each):
            at = before + step * each + k
            matrix = circulant[pl.ds(starts[at], TILE), :].astype(jnp.bfloat16)
            tile = got[step * each + k, pl.ds(first_row, rows_here), :]
            tile = jnp.where(scales[at] > 0.0, tile, jnp.zeros_like(tile))
            product = jnp.dot(tile, matrix, preferred_element_type=jnp.float32)
            products.append(product * scales[at])
        for k in range(each):
            target = targets[before + step * each + k]
            total[target] = total[target] + products[k]
        return carry

    before = 0
    for got in arrived:
        each = min(ARRIVALS, got.shape[0])
        lax.fori_loop(0, got.shape[0] // each, partial(group_step, got, before, each), 0)
        before += got.shape[0]
    out[...] = total[...].astype(out.dtype)


def gathered(block, axis_name):
    peers = lax.axis_size(axis_name)
    if peers & (peers - 1):
        return lax.all_gather(block, axis_name, axis=0, tiled=True)
    me = lax.axis_index(axis_name)
    step = 1
    while step < peers:
        other = lax.ppermute(block, axis_name, [(i, i ^ step) for i in range(peers)])
        lower = (me & step) == 0
        block = jnp.where(
            lower, jnp.concatenate([block, other], axis=0), jnp.concatenate([other, block], axis=0)
        )
        step *= 2
    return block


def arrivals(owner, details, everything):
    senders, _, tile_count = details.shape
    slot_count = senders * CAP
    here = owner * CAP + jnp.arange(CAP, dtype=jnp.int32)
    match = (details[:, None, 0, :] == here[None, :, None]).reshape(slot_count, 1, tile_count)
    fields = jnp.repeat(details[:, 1:], CAP, axis=0).reshape(slot_count, 3, tile_count)
    chosen = jnp.sum(jnp.where(match, fields, 0), axis=2)
    map_iota = jnp.arange(MAP_DEV, dtype=jnp.int32)
    owned = jnp.where(everything[:, 0] // CAP == owner, everything[:, 3], 0).astype(jnp.float32)
    on_map = everything[:, 1][None] == map_iota[:, None, None]
    sums = jnp.sum(jnp.where(on_map, owned[None], 0.0), axis=(1, 2))
    inverse = 1.0 / jnp.maximum(sums, 1.0)
    picked = chosen[:, 0][:, None] == map_iota[None, :]
    scales = jnp.sum(jnp.where(picked, inverse[None, :], 0.0), axis=1) * chosen[:, 2].astype(jnp.float32)
    return chosen[:, 0], (TILE - chosen[:, 1]) & (TILE - 1), scales


def map_sum(lists, rounded_kernel, tiles, kind, name, first_row, rows_here):
    extent = (MAP_DEV, rows_here, TILE)
    tiles = tiles if isinstance(tiles, (list, tuple)) else [tiles]
    return pl.pallas_call(
        partial(map_kernel, first_row=first_row),
        out_shape=jax.ShapeDtypeStruct(extent, kind),
        in_specs=[SMEM] * 4 + [VMEM] * len(tiles),
        out_specs=VMEM,
        scratch_shapes=[pltpu.VMEM((2 * TILE, TILE), jnp.float32), pltpu.VMEM(extent, jnp.float32)],
        compiler_params=params,
        name=name,
    )(*lists, rounded_kernel, *tiles)


def shards(
    radar_stack,
    filter_taps,
    filter_lengths,
    resample_kernel,
    tile_owner,
    map_slot,
    correlation,
    offsets,
):
    peers = lax.axis_size("date")
    me = lax.axis_index("date")
    _, dates_here, rows_count, ranges_count = radar_stack.shape
    dates = dates_here * peers
    line_count = rows_count // peers
    sides = ranges_count // TILE
    tile_count = line_count * sides
    slot_count = peers * CAP
    window_count = (line_count // PATCH_AZ) * (ranges_count // PATCH_RG)
    assert line_count == PATCH_AZ

    sent = pl.pallas_call(
        filter_kernel,
        out_shape=pltpu.HBM((rows_count * 2 * dates_here, ranges_count), jnp.bfloat16),
        in_specs=[HBM, HBM, HBM],
        out_specs=HBM,
        scratch_shapes=[
            pltpu.SMEM((dates_here,), jnp.int32),
            pltpu.VMEM(filter_taps.shape, jnp.float32),
            pltpu.VMEM((dates_here, 2, rows_count, ranges_count), jnp.bfloat16),
            pltpu.VMEM((sides, rows_count * 2 * dates_here, TILE), jnp.float32),
            pltpu.VMEM((rows_count * 2 * dates_here, ranges_count), jnp.bfloat16),
            pltpu.SemaphoreType.DMA((dates_here + 2,)),
            pltpu.SemaphoreType.DMA((PIECES,)),
        ],
        compiler_params=wide_params,
        name="filter",
    )(filter_lengths, filter_taps, radar_stack)
    sent, tile_owner, map_slot, correlation, offsets = lax.optimization_barrier(
        (sent, tile_owner, map_slot, correlation, offsets)
    )
    owners = tile_owner[:, 0]
    tile_iota = jnp.arange(tile_count, dtype=jnp.int32)
    starts_here = offsets + PATCH_RG * (tile_iota // sides)
    earlier = jnp.logical_and(
        owners[:, None] == owners[None, :], tile_iota[None, :] < tile_iota[:, None]
    )
    half = peers // 2
    ranks = jnp.sum(earlier, axis=1).astype(jnp.int32)
    step = (owners % half) ^ (me % half)
    leaves = owners // half != me // half
    slots = jnp.where(leaves, owners % half, step // 2) * CAP + ranks
    routes = jnp.where(leaves, 0, 1 + step % 2)
    details = jnp.stack([owners * CAP + ranks, map_slot, starts_here, correlation], axis=0)[None]
    sent = sent.reshape(peers, line_count * 2 * dates_here, ranges_count)
    got_lines = lax.all_to_all(sent, "date", split_axis=0, concat_axis=0, tiled=True)
    all_details = gathered(details, "date")
    got_lines, all_details = lax.optimization_barrier((got_lines, all_details))

    mixed = dates_here == 8 and peers % 2 == 0
    got_lines = got_lines.reshape(peers, line_count, 2 * dates_here, ranges_count)
    if not mixed:
        got_lines = got_lines.reshape(peers, line_count, 2, dates_here, ranges_count)
        got_lines = got_lines.transpose(1, 2, 0, 3, 4).reshape(1, line_count, 2 * dates, ranges_count)
    slot_count = half * CAP
    buffer = pltpu.HBM((slot_count, 2 * dates, TILE), jnp.bfloat16)
    near_buffer = pltpu.HBM((slot_count // 2, 2 * dates, TILE), jnp.bfloat16)
    leaving, same, other = pl.pallas_call(
        partial(whiten_kernel, mixed=mixed),
        out_shape=(buffer, near_buffer, near_buffer),
        in_specs=[SMEM, SMEM, VMEM],
        out_specs=(HBM, HBM, HBM),
        scratch_shapes=[
            pltpu.VMEM((window_count, 2 * dates, TILE), jnp.bfloat16),
            pltpu.VMEM((tile_count, 2 * dates, TILE), jnp.bfloat16),
            pltpu.SemaphoreType.DMA((tile_count,)),
        ],
        compiler_params=params,
        name="whiten",
    )(slots, routes, got_lines)
    other = lax.ppermute(other, "date", [(i, i ^ 1) for i in range(peers)])
    other, all_details, resample_kernel = lax.optimization_barrier(
        (other, all_details, resample_kernel)
    )
    halves = [list(range(half)), list(range(half, peers))]

    def within_half(tiles):
        return lax.all_to_all(
            tiles, "date", split_axis=0, concat_axis=0, axis_index_groups=halves, tiled=True
        )

    rounded_kernel = lax.optimization_barrier(resample_kernel.astype(jnp.bfloat16)).astype(jnp.float32)
    near = lax.dynamic_slice_in_dim(all_details, me // half * half, half, axis=0)
    gathered_here = within_half(leaving)
    far_lists = arrivals((me + half) % peers, near, all_details)
    senders = jnp.arange(half, dtype=jnp.int32) ^ (me % half)
    near_lists = arrivals(me, jnp.take(near, senders, axis=0), all_details)
    gathered_here, far_lists, near_lists, rounded_kernel = lax.optimization_barrier(
        (gathered_here, far_lists, near_lists, rounded_kernel)
    )
    near_tiles = []
    for k in range(half // 2):
        pair = jnp.concatenate([same[k * CAP : (k + 1) * CAP], other[k * CAP : (k + 1) * CAP]], axis=0)
        if k:
            pair = lax.ppermute(pair, "date", [(i, i ^ (2 * k)) for i in range(peers)])
        near_tiles.append(pair)
    across = [(i, (i + half) % peers) for i in range(peers)]
    rows_each = 2 * dates // HALVES
    from_far = []
    for piece in range(HALVES):
        partial_sums = map_sum(
            far_lists, rounded_kernel, gathered_here, jnp.bfloat16, "far_sum", piece * rows_each, rows_each
        )
        if piece + 1 < HALVES:
            partial_sums, gathered_here = lax.optimization_barrier((partial_sums, gathered_here))
        from_far.append(lax.ppermute(partial_sums, "date", across))
    own_sums = map_sum(
        near_lists, rounded_kernel, near_tiles, jnp.float32, "near_sum", 0, 2 * dates
    )
    return own_sums + jnp.concatenate(from_far, axis=1).astype(jnp.float32)


def solution(mesh):
    in_specs = (
        P(None, "date", "grp", None),
        P(None, "date", None),
        P("date"),
        P(),
        P(("grp", "date"), None),
        P(("grp", "date")),
        P(("grp", "date")),
        P(("grp", "date")),
    )
    out_specs = P(("grp", "date"), None, None)
    return jax.shard_map(shards, mesh=mesh, in_specs=in_specs, out_specs=out_specs, check_vma=False)
```

```python
from functools import partial

import jax
import jax.numpy as jnp
from jax import lax
from jax.experimental import pallas as pl
from jax.experimental.pallas import tpu as pltpu
from jax.sharding import PartitionSpec as P

PATCH_AZ = 8
PATCH_RG = 16
TILE = 128
KW = 4
CAP = 2
MAP_DEV = 8
GROUP = 16
PIECES = 4
ARRIVALS = 8
TIED = 1

diag_load = 0.5
small_eps = 1e-05
VMEM = pl.BlockSpec(memory_space=pltpu.VMEM)
SMEM = pl.BlockSpec(memory_space=pltpu.SMEM)
HBM = pl.BlockSpec(memory_space=pltpu.HBM)
MIB = 1024 * 1024
params = pltpu.CompilerParams(vmem_limit_bytes=32 * MIB)
wide_params = pltpu.CompilerParams(vmem_limit_bytes=60 * MIB)


def filter_kernel(lengths_hbm, taps_hbm, radar, sent, lengths, taps, columns, staged, rounded, sems, out_sems):
    _, dates_here, rows_count, ranges_count = radar.shape
    tap_count = taps.shape[2]
    period = rows_count + tap_count
    copy_lengths = pltpu.make_async_copy(lengths_hbm, lengths, sems.at[dates_here])
    copy_taps = pltpu.make_async_copy(taps_hbm, taps, sems.at[dates_here + 1])
    copies = [
        pltpu.make_async_copy(radar.at[:, date], columns.at[date], sems.at[date])
        for date in range(dates_here)
    ]
    copy_lengths.start()
    copy_taps.start()
    for copy in copies:
        copy.start()
    copy_lengths.wait()
    copy_taps.wait()
    position = lax.broadcasted_iota(jnp.int32, (1, tap_count), 1)
    operators = []
    for date in range(dates_here):
        mats = []
        for part in range(2):
            used = jnp.where(position < lengths[date], taps[part, pl.ds(date, 1), :], 0.0)
            padded = jnp.concatenate([used, jnp.zeros((1, period - tap_count), jnp.float32)], axis=1)
            spread = jnp.broadcast_to(padded, (rows_count, period))
            rolled = pltpu.roll(spread, period - tap_count // 2, 1, stride=1, stride_axis=0)
            mats.append(rolled[:, :rows_count].astype(jnp.bfloat16))
        operators.append(mats)
    for copy in copies:
        copy.wait()
    for date, (real_mat, imag_mat) in enumerate(operators):
        cells = columns[date].reshape(2 * rows_count, ranges_count)
        for part, halves in enumerate(((real_mat, -imag_mat), (imag_mat, real_mat))):
            operator = jnp.concatenate(halves, axis=1)
            product = jnp.dot(operator, cells, preferred_element_type=jnp.float32)
            for side in range(ranges_count // TILE):
                skewed = pltpu.roll(
                    product[:, side * TILE : (side + 1) * TILE], 0, 1, stride=PATCH_RG, stride_axis=0
                )
                first = part * dates_here + date
                staged[side, pl.ds(first, rows_count, stride=2 * dates_here), :] = skewed
    total = sent.shape[0]
    pieces = []
    for piece in range(PIECES):
        rows = pl.ds(piece * (total // PIECES), total // PIECES)
        for side in range(ranges_count // TILE):
            rounded[rows, side * TILE : (side + 1) * TILE] = staged[side, rows, :].astype(jnp.bfloat16)
        pieces.append(pltpu.make_async_copy(rounded.at[rows], sent.at[rows], out_sems.at[piece]))
        pieces[-1].start()
    for piece in pieces:
        piece.wait()


def barrel(blocks, lane_block):
    count = len(blocks)
    step = 1
    while step < count:
        taken = (lane_block & step) != 0
        blocks = [jnp.where(taken, blocks[(i + step) % count], blocks[i]) for i in range(count)]
        step *= 2
    return blocks


def embedded(real_part, imag_part):
    upper = jnp.concatenate([real_part, -imag_part], axis=1)
    lower = jnp.concatenate([imag_part, real_part], axis=1)
    return jnp.concatenate([upper, lower], axis=0)


def whiten_group(cells):
    dates, looks = cells[0].shape[0] // 2, cells[0].shape[1]
    row = lax.broadcasted_iota(jnp.int32, (dates, dates), 0)
    col = lax.broadcasted_iota(jnp.int32, (dates, dates), 1)
    diagonal = row == col
    grams = []
    for cell in cells:
        real_part, imag_part = cell[:dates], cell[dates:]
        straight = jnp.concatenate([real_part, imag_part], axis=1)
        turned = jnp.concatenate([imag_part, -real_part], axis=1)
        left = jnp.concatenate([straight, turned], axis=0)
        grams.append(
            lax.dot_general(left, straight, (((1,), (1,)), ((), ())), preferred_element_type=jnp.float32)
        )
    scaled, bounds = [], []
    for gram in grams:
        gram_re, gram_im = gram[:dates], gram[dates:]
        power = jnp.where(diagonal, gram_re, 0.0)
        row_scale = lax.rsqrt(jnp.sum(power, axis=1, keepdims=True) * (1.0 / looks) + small_eps)
        col_scale = lax.rsqrt(jnp.sum(power, axis=0, keepdims=True) * (1.0 / looks) + small_eps)
        col_scale = col_scale * (1.0 / looks)
        size = (jnp.abs(gram_re) + jnp.abs(gram_im)) * row_scale
        sums = jnp.sum(size, axis=0, keepdims=True) * col_scale + diag_load
        inv_bound = 1.0 / jnp.max(sums, axis=1, keepdims=True)
        factor = row_scale * (col_scale * inv_bound)
        load = jnp.where(diagonal, diag_load * inv_bound, 0.0)
        scaled.append(jnp.concatenate([gram_re * factor + load, gram_im * factor], axis=0))
        bounds.append(inv_bound)
    values = [cell.astype(jnp.float32) for cell in cells]
    rounded = list(cells)
    for sweep in range(2):
        mats = [s.astype(jnp.bfloat16) for s in scaled]
        products = [
            jnp.dot(
                embedded(m[:dates], m[dates:]),
                jnp.concatenate([m, r], axis=1),
                preferred_element_type=jnp.float32,
            )
            for m, r in zip(mats, rounded)
        ]
        scaled = [2.0 * s - p[:, :dates] for s, p in zip(scaled, products)]
        values = [2.0 * v - p[:, dates:] for v, p in zip(values, products)]
        rounded = [v.astype(jnp.bfloat16) for v in values]
    mats = [s.astype(jnp.bfloat16) for s in scaled]
    products = [
        jnp.dot(embedded(m[:dates], m[dates:]), r, preferred_element_type=jnp.float32)
        for m, r in zip(mats, rounded)
    ]
    return [
        ((2.0 * v - p) * b).astype(jnp.bfloat16) for v, p, b in zip(values, products, bounds)
    ]


def whiten_kernel(slots, routes, lines, *refs, mixed):
    *buffers, windows, tiles, sems = refs
    senders, line_count, part_rows, ranges_count = lines.shape
    dates = windows.shape[1] // 2
    sides = ranges_count // TILE
    lane_block = lax.broadcasted_iota(jnp.int32, (1, TILE), 1) // PATCH_RG
    per_side = TILE // PATCH_RG
    for side in range(sides):
        lanes = pl.ds(side * TILE, TILE)
        if mixed:
            half = part_rows // 2
            for first in range(0, senders, 2):
                blocks = [
                    lines[first : first + 2, a, :, lanes].astype(jnp.float32) for a in range(line_count)
                ]
                found = barrel(blocks, lane_block[:, None])
                rows = pl.ds(first * half, 2 * half)
                rows_im = pl.ds(dates + first * half, 2 * half)
                for w in range(per_side):
                    block = found[-w % per_side]
                    real_part = block[:, :half].reshape(2 * half, TILE)
                    imag_part = block[:, half:].reshape(2 * half, TILE)
                    windows[side * per_side + w, rows, :] = real_part.astype(jnp.bfloat16)
                    windows[side * per_side + w, rows_im, :] = imag_part.astype(jnp.bfloat16)
        else:
            for first in range(0, 2 * dates, 16):
                rows = pl.ds(first, 16)
                blocks = [lines[0, a, rows, lanes].astype(jnp.float32) for a in range(line_count)]
                found = barrel(blocks, lane_block)
                for w in range(per_side):
                    windows[side * per_side + w, rows, :] = found[-w % per_side].astype(jnp.bfloat16)

    def group_step(step, carry):
        first = step * GROUP
        results = whiten_group([windows[first + k] for k in range(GROUP)])
        for k in range(GROUP):
            windows[first + k] = results[k]
        return carry

    lax.fori_loop(0, windows.shape[0] // GROUP, group_step, 0)
    copies = []
    for side in range(sides):
        for first in range(0, 2 * dates, 16):
            rows = pl.ds(first, 16)
            blocks = [
                windows[side * per_side + w, rows, :].astype(jnp.float32) for w in range(per_side)
            ]
            found = barrel(blocks, lane_block)
            for a in range(line_count):
                tiles[a * sides + side, rows, :] = found[-a % per_side].astype(jnp.bfloat16)
        for a in range(line_count):
            at = a * sides + side
            routed = [
                pltpu.make_async_copy(tiles.at[at], buffer.at[slots[at]], sems.at[at])
                for buffer in buffers
            ]
            for route, copy in enumerate(routed):
                pl.when(routes[at] == route)(copy.start)
            copies.append(routed[0])
    for copy in copies:
        copy.wait()


def map_kernel(targets, starts, scales, kernel, *refs, arrays, first_slot):
    arrived, rest = refs[:arrays], list(refs[arrays:])
    total = rest.pop() if rest[-1].shape[0] == MAP_DEV else None
    *begun, out, circulant = rest
    total = out if total is None else total
    source = lax.broadcasted_iota(jnp.int32, circulant.shape, 0)
    column = lax.broadcasted_iota(jnp.int32, circulant.shape, 1)
    lag = (source - column) & (TILE - 1)
    taps = jnp.zeros(circulant.shape, jnp.float32)
    for k in range(KW):
        taps = jnp.where(lag == k, kernel[k], taps)
    circulant[...] = taps
    if begun:
        total[...] = sum(sums[...].astype(jnp.float32) for sums in begun)
    else:
        total[...] = jnp.zeros(total.shape, jnp.float32)
    jobs = [(got, k) for got in arrived for k in range(got.shape[0])]
    for first in range(0, len(jobs), ARRIVALS):
        products = []
        for k, (got, place) in enumerate(jobs[first : first + ARRIVALS]):
            at = first_slot + first + k
            matrix = circulant[pl.ds(starts[at], TILE), :].astype(jnp.bfloat16)
            tile = got[place]
            tile = jnp.where(scales[at] > 0.0, tile, jnp.zeros_like(tile))
            products.append(jnp.dot(tile, matrix, preferred_element_type=jnp.float32) * scales[at])
        for k, product in enumerate(products):
            target = targets[first_slot + first + k]
            total[target] = total[target] + product
    if total is not out:
        out[...] = total[...].astype(out.dtype)


def gathered(block, axis_name):
    peers = lax.axis_size(axis_name)
    if peers & (peers - 1):
        return lax.all_gather(block, axis_name, axis=0, tiled=True)
    me = lax.axis_index(axis_name)
    step = 1
    while step < peers:
        other = lax.ppermute(block, axis_name, [(i, i ^ step) for i in range(peers)])
        lower = (me & step) == 0
        block = jnp.where(
            lower, jnp.concatenate([block, other], axis=0), jnp.concatenate([other, block], axis=0)
        )
        step *= 2
    return block


def arrivals(owner, details, everything):
    senders, _, tile_count = details.shape
    slot_count = senders * CAP
    here = owner * CAP + jnp.arange(CAP, dtype=jnp.int32)
    match = (details[:, None, 0, :] == here[None, :, None]).reshape(slot_count, 1, tile_count)
    fields = jnp.repeat(details[:, 1:], CAP, axis=0).reshape(slot_count, 3, tile_count)
    chosen = jnp.sum(jnp.where(match, fields, 0), axis=2)
    map_iota = jnp.arange(MAP_DEV, dtype=jnp.int32)
    owned = jnp.where(everything[:, 0] // CAP == owner, everything[:, 3], 0).astype(jnp.float32)
    on_map = everything[:, 1][None] == map_iota[:, None, None]
    sums = jnp.sum(jnp.where(on_map, owned[None], 0.0), axis=(1, 2))
    inverse = 1.0 / jnp.maximum(sums, 1.0)
    picked = chosen[:, 0][:, None] == map_iota[None, :]
    scales = jnp.sum(jnp.where(picked, inverse[None, :], 0.0), axis=1) * chosen[:, 2].astype(jnp.float32)
    return chosen[:, 0], (TILE - chosen[:, 1]) & (TILE - 1), scales


def map_sum(lists, rounded_kernel, tiles, kind, name, first_slot, begun=()):
    extent = (MAP_DEV,) + tiles[0].shape[1:]
    scratch = [pltpu.VMEM((2 * TILE, TILE), jnp.float32)]
    if kind != jnp.float32:
        scratch.append(pltpu.VMEM(extent, jnp.float32))
    return pl.pallas_call(
        partial(map_kernel, arrays=len(tiles), first_slot=first_slot),
        out_shape=jax.ShapeDtypeStruct(extent, kind),
        in_specs=[SMEM] * 4 + [VMEM] * (len(tiles) + len(begun)),
        out_specs=VMEM,
        scratch_shapes=scratch,
        compiler_params=params,
        name=name,
    )(*lists, rounded_kernel, *tiles, *begun)


def shards(
    radar_stack,
    filter_taps,
    filter_lengths,
    resample_kernel,
    tile_owner,
    map_slot,
    correlation,
    offsets,
):
    peers = lax.axis_size("date")
    me = lax.axis_index("date")
    _, dates_here, rows_count, ranges_count = radar_stack.shape
    dates = dates_here * peers
    line_count = rows_count // peers
    sides = ranges_count // TILE
    tile_count = line_count * sides
    slot_count = peers * CAP
    window_count = (line_count // PATCH_AZ) * (ranges_count // PATCH_RG)
    assert line_count == PATCH_AZ

    sent = pl.pallas_call(
        filter_kernel,
        out_shape=pltpu.HBM((rows_count * 2 * dates_here, ranges_count), jnp.bfloat16),
        in_specs=[HBM, HBM, HBM],
        out_specs=HBM,
        scratch_shapes=[
            pltpu.SMEM((dates_here,), jnp.int32),
            pltpu.VMEM(filter_taps.shape, jnp.float32),
            pltpu.VMEM((dates_here, 2, rows_count, ranges_count), jnp.bfloat16),
            pltpu.VMEM((sides, rows_count * 2 * dates_here, TILE), jnp.float32),
            pltpu.VMEM((rows_count * 2 * dates_here, ranges_count), jnp.bfloat16),
            pltpu.SemaphoreType.DMA((dates_here + 2,)),
            pltpu.SemaphoreType.DMA((PIECES,)),
        ],
        compiler_params=wide_params,
        name="filter",
    )(filter_lengths, filter_taps, radar_stack)
    sent, tile_owner, map_slot, correlation, offsets = lax.optimization_barrier(
        (sent, tile_owner, map_slot, correlation, offsets)
    )
    owners = tile_owner[:, 0]
    tile_iota = jnp.arange(tile_count, dtype=jnp.int32)
    starts_here = offsets + PATCH_RG * (tile_iota // sides)
    earlier = jnp.logical_and(
        owners[:, None] == owners[None, :], tile_iota[None, :] < tile_iota[:, None]
    )
    half = peers // 2
    ranks = jnp.sum(earlier, axis=1).astype(jnp.int32)
    step = (owners % half) ^ (me % half)
    leaves = owners // half != me // half
    slots = step // 2 * CAP + ranks
    routes = jnp.where(leaves, 0, 2) + step % 2
    details = jnp.stack([owners * CAP + ranks, map_slot, starts_here, correlation], axis=0)[None]
    sent = sent.reshape(peers, line_count * 2 * dates_here, ranges_count)
    got_lines = lax.all_to_all(sent, "date", split_axis=0, concat_axis=0, tiled=True)
    all_details = gathered(details, "date")
    got_lines, all_details = lax.optimization_barrier((got_lines, all_details))

    mixed = dates_here == 8 and peers % 2 == 0
    got_lines = got_lines.reshape(peers, line_count, 2 * dates_here, ranges_count)
    if not mixed:
        got_lines = got_lines.reshape(peers, line_count, 2, dates_here, ranges_count)
        got_lines = got_lines.transpose(1, 2, 0, 3, 4).reshape(1, line_count, 2 * dates, ranges_count)
    buffer = pltpu.HBM((half // 2 * CAP, 2 * dates, TILE), jnp.bfloat16)
    leaving_same, leaving_other, same, other = pl.pallas_call(
        partial(whiten_kernel, mixed=mixed),
        out_shape=(buffer,) * 4,
        in_specs=[SMEM, SMEM, VMEM],
        out_specs=(HBM,) * 4,
        scratch_shapes=[
            pltpu.VMEM((window_count, 2 * dates, TILE), jnp.bfloat16),
            pltpu.VMEM((tile_count, 2 * dates, TILE), jnp.bfloat16),
            pltpu.SemaphoreType.DMA((tile_count,)),
        ],
        compiler_params=params,
        name="whiten",
    )(slots, routes, got_lines)

    def exchanged(values, step):
        return lax.ppermute(values, "date", [(i, i ^ step) for i in range(peers)])

    def from_chips(mine, received):
        tiles = []
        for k in range(half // 2):
            at = slice(k * CAP, (k + 1) * CAP)
            tiles += [exchanged(cells[at], 2 * k) if k else cells[at] for cells in (mine, received)]
        return tiles

    early = half // 2
    early_slots = early * CAP
    far_tiles = from_chips(leaving_same, exchanged(leaving_other, 1))
    other = exchanged(other, 1)
    other, all_details, resample_kernel = lax.optimization_barrier(
        (other, all_details, resample_kernel)
    )
    rounded_kernel = lax.optimization_barrier(resample_kernel.astype(jnp.bfloat16)).astype(jnp.float32)
    senders = jnp.arange(half, dtype=jnp.int32) ^ (me % half)
    near = jnp.take(all_details, me // half * half + senders, axis=0)
    far_lists = arrivals((me + half) % peers, near, all_details)
    near_lists = arrivals(me, near, all_details)
    far_begun = map_sum(far_lists, rounded_kernel, far_tiles[:early], jnp.float32, "far_early", 0)
    partial_sums = map_sum(
        far_lists, rounded_kernel, far_tiles[early:], jnp.bfloat16, "far_late", early_slots, [far_begun]
    )
    partial_sums, same, other, near_lists = lax.optimization_barrier(
        (partial_sums, same, other, near_lists)
    )
    from_far = lax.ppermute(partial_sums, "date", [(i, (i + half) % peers) for i in range(peers)])
    near_tiles = from_chips(same, other)
    near_begun = map_sum(near_lists, rounded_kernel, near_tiles[:early], jnp.float32, "near_early", 0)
    return map_sum(
        near_lists,
        rounded_kernel,
        near_tiles[early:],
        jnp.float32,
        "near_late",
        early_slots,
        [near_begun, from_far],
    )


def solution(mesh):
    in_specs = (
        P(None, "date", "grp", None),
        P(None, "date", None),
        P("date"),
        P(),
        P(("grp", "date"), None),
        P(("grp", "date")),
        P(("grp", "date")),
        P(("grp", "date")),
    )
    out_specs = P(("grp", "date"), None, None)
    return jax.shard_map(shards, mesh=mesh, in_specs=in_specs, out_specs=out_specs, check_vma=False)
```

```python
from functools import partial

import jax
import jax.numpy as jnp
from jax import lax
from jax.experimental import pallas as pl
from jax.experimental.pallas import tpu as pltpu
from jax.sharding import PartitionSpec as P

PATCH_AZ = 8
PATCH_RG = 16
TILE = 128
KW = 4
CAP = 2
MAP_DEV = 8
GROUP = 16
PIECES = 4
ARRIVALS = 8
TIED = 1

diag_load = 0.5
small_eps = 1e-05
VMEM = pl.BlockSpec(memory_space=pltpu.VMEM)
SMEM = pl.BlockSpec(memory_space=pltpu.SMEM)
HBM = pl.BlockSpec(memory_space=pltpu.HBM)
MIB = 1024 * 1024
params = pltpu.CompilerParams(vmem_limit_bytes=32 * MIB)
wide_params = pltpu.CompilerParams(vmem_limit_bytes=60 * MIB)


def filter_kernel(lengths_hbm, taps_hbm, radar, sent, lengths, taps, columns, staged, rounded, sems, out_sems):
    _, dates_here, rows_count, ranges_count = radar.shape
    tap_count = taps.shape[2]
    period = rows_count + tap_count
    copy_lengths = pltpu.make_async_copy(lengths_hbm, lengths, sems.at[dates_here])
    copy_taps = pltpu.make_async_copy(taps_hbm, taps, sems.at[dates_here + 1])
    copies = [
        pltpu.make_async_copy(radar.at[:, date], columns.at[date], sems.at[date])
        for date in range(dates_here)
    ]
    copy_lengths.start()
    copy_taps.start()
    for copy in copies:
        copy.start()
    copy_lengths.wait()
    copy_taps.wait()
    position = lax.broadcasted_iota(jnp.int32, (1, tap_count), 1)
    operators = []
    for date in range(dates_here):
        mats = []
        for part in range(2):
            used = jnp.where(position < lengths[date], taps[part, pl.ds(date, 1), :], 0.0)
            padded = jnp.concatenate([used, jnp.zeros((1, period - tap_count), jnp.float32)], axis=1)
            spread = jnp.broadcast_to(padded, (rows_count, period))
            rolled = pltpu.roll(spread, period - tap_count // 2, 1, stride=1, stride_axis=0)
            mats.append(rolled[:, :rows_count].astype(jnp.bfloat16))
        operators.append(mats)
    for copy in copies:
        copy.wait()
    for date, (real_mat, imag_mat) in enumerate(operators):
        cells = columns[date].reshape(2 * rows_count, ranges_count)
        for part, halves in enumerate(((real_mat, -imag_mat), (imag_mat, real_mat))):
            operator = jnp.concatenate(halves, axis=1)
            product = jnp.dot(operator, cells, preferred_element_type=jnp.float32)
            for side in range(ranges_count // TILE):
                skewed = pltpu.roll(
                    product[:, side * TILE : (side + 1) * TILE], 0, 1, stride=PATCH_RG, stride_axis=0
                )
                first = part * dates_here + date
                staged[side, pl.ds(first, rows_count, stride=2 * dates_here), :] = skewed
    total = sent.shape[0]
    pieces = []
    for piece in range(PIECES):
        rows = pl.ds(piece * (total // PIECES), total // PIECES)
        for side in range(ranges_count // TILE):
            rounded[rows, side * TILE : (side + 1) * TILE] = staged[side, rows, :].astype(jnp.bfloat16)
        pieces.append(pltpu.make_async_copy(rounded.at[rows], sent.at[rows], out_sems.at[piece]))
        pieces[-1].start()
    for piece in pieces:
        piece.wait()


def barrel(blocks, lane_block):
    count = len(blocks)
    step = 1
    while step < count:
        taken = (lane_block & step) != 0
        blocks = [jnp.where(taken, blocks[(i + step) % count], blocks[i]) for i in range(count)]
        step *= 2
    return blocks


def embedded(real_part, imag_part):
    upper = jnp.concatenate([real_part, -imag_part], axis=1)
    lower = jnp.concatenate([imag_part, real_part], axis=1)
    return jnp.concatenate([upper, lower], axis=0)


def whiten_group(cells):
    dates, looks = cells[0].shape[0] // 2, cells[0].shape[1]
    row = lax.broadcasted_iota(jnp.int32, (dates, dates), 0)
    col = lax.broadcasted_iota(jnp.int32, (dates, dates), 1)
    diagonal = row == col
    grams = []
    for cell in cells:
        real_part, imag_part = cell[:dates], cell[dates:]
        straight = jnp.concatenate([real_part, imag_part], axis=1)
        turned = jnp.concatenate([imag_part, -real_part], axis=1)
        left = jnp.concatenate([straight, turned], axis=0)
        grams.append(
            lax.dot_general(left, straight, (((1,), (1,)), ((), ())), preferred_element_type=jnp.float32)
        )
    scaled, bounds = [], []
    for gram in grams:
        gram_re, gram_im = gram[:dates], gram[dates:]
        power = jnp.where(diagonal, gram_re, 0.0)
        row_scale = lax.rsqrt(jnp.sum(power, axis=1, keepdims=True) * (1.0 / looks) + small_eps)
        col_scale = lax.rsqrt(jnp.sum(power, axis=0, keepdims=True) * (1.0 / looks) + small_eps)
        col_scale = col_scale * (1.0 / looks)
        size = (jnp.abs(gram_re) + jnp.abs(gram_im)) * row_scale
        sums = jnp.sum(size, axis=0, keepdims=True) * col_scale + diag_load
        inv_bound = 1.0 / jnp.max(sums, axis=1, keepdims=True)
        factor = row_scale * (col_scale * inv_bound)
        load = jnp.where(diagonal, diag_load * inv_bound, 0.0)
        scaled.append(jnp.concatenate([gram_re * factor + load, gram_im * factor], axis=0))
        bounds.append(inv_bound)
    values = [cell.astype(jnp.float32) for cell in cells]
    rounded = list(cells)
    for sweep in range(2):
        mats = [s.astype(jnp.bfloat16) for s in scaled]
        products = [
            jnp.dot(
                embedded(m[:dates], m[dates:]),
                jnp.concatenate([m, r], axis=1),
                preferred_element_type=jnp.float32,
            )
            for m, r in zip(mats, rounded)
        ]
        scaled = [2.0 * s - p[:, :dates] for s, p in zip(scaled, products)]
        values = [2.0 * v - p[:, dates:] for v, p in zip(values, products)]
        rounded = [v.astype(jnp.bfloat16) for v in values]
    mats = [s.astype(jnp.bfloat16) for s in scaled]
    products = [
        jnp.dot(embedded(m[:dates], m[dates:]), r, preferred_element_type=jnp.float32)
        for m, r in zip(mats, rounded)
    ]
    return [
        ((2.0 * v - p) * b).astype(jnp.bfloat16) for v, p, b in zip(values, products, bounds)
    ]


def whiten_kernel(slots, routes, lines, *refs, mixed):
    *buffers, windows, tiles, sems = refs
    senders, line_count, part_rows, ranges_count = lines.shape
    dates = windows.shape[1] // 2
    sides = ranges_count // TILE
    lane_block = lax.broadcasted_iota(jnp.int32, (1, TILE), 1) // PATCH_RG
    per_side = TILE // PATCH_RG
    for side in range(sides):
        lanes = pl.ds(side * TILE, TILE)
        if mixed:
            half = part_rows // 2
            for first in range(0, senders, 2):
                blocks = [
                    lines[first : first + 2, a, :, lanes].astype(jnp.float32) for a in range(line_count)
                ]
                found = barrel(blocks, lane_block[:, None])
                rows = pl.ds(first * half, 2 * half)
                rows_im = pl.ds(dates + first * half, 2 * half)
                for w in range(per_side):
                    block = found[-w % per_side]
                    real_part = block[:, :half].reshape(2 * half, TILE)
                    imag_part = block[:, half:].reshape(2 * half, TILE)
                    windows[side * per_side + w, rows, :] = real_part.astype(jnp.bfloat16)
                    windows[side * per_side + w, rows_im, :] = imag_part.astype(jnp.bfloat16)
        else:
            for first in range(0, 2 * dates, 16):
                rows = pl.ds(first, 16)
                blocks = [lines[0, a, rows, lanes].astype(jnp.float32) for a in range(line_count)]
                found = barrel(blocks, lane_block)
                for w in range(per_side):
                    windows[side * per_side + w, rows, :] = found[-w % per_side].astype(jnp.bfloat16)

    def group_step(step, carry):
        first = step * GROUP
        results = whiten_group([windows[first + k] for k in range(GROUP)])
        for k in range(GROUP):
            windows[first + k] = results[k]
        return carry

    lax.fori_loop(0, windows.shape[0] // GROUP, group_step, 0)
    copies = []
    for side in range(sides):
        for first in range(0, 2 * dates, 16):
            rows = pl.ds(first, 16)
            blocks = [
                windows[side * per_side + w, rows, :].astype(jnp.float32) for w in range(per_side)
            ]
            found = barrel(blocks, lane_block)
            for a in range(line_count):
                tiles[a * sides + side, rows, :] = found[-a % per_side].astype(jnp.bfloat16)
        for a in range(line_count):
            at = a * sides + side
            routed = [
                pltpu.make_async_copy(tiles.at[at], buffer.at[slots[at]], sems.at[at])
                for buffer in buffers
            ]
            for route, copy in enumerate(routed):
                pl.when(routes[at] == route)(copy.start)
            copies.append(pltpu.make_async_copy(tiles.at[at], buffers[0].at[0], sems.at[at]))
    for copy in copies:
        copy.wait()


def map_kernel(targets, starts, scales, kernel, *refs, arrays, first_slot):
    arrived, rest = refs[:arrays], list(refs[arrays:])
    total = rest.pop() if rest[-1].shape[0] == MAP_DEV else None
    *begun, out, circulant = rest
    total = out if total is None else total
    source = lax.broadcasted_iota(jnp.int32, circulant.shape, 0)
    column = lax.broadcasted_iota(jnp.int32, circulant.shape, 1)
    lag = (source - column) & (TILE - 1)
    taps = jnp.zeros(circulant.shape, jnp.float32)
    for k in range(KW):
        taps = jnp.where(lag == k, kernel[k], taps)
    circulant[...] = taps
    if begun:
        total[...] = sum(sums[...].astype(jnp.float32) for sums in begun)
    else:
        total[...] = jnp.zeros(total.shape, jnp.float32)
    jobs = [(got, k) for got in arrived for k in range(got.shape[0])]
    for first in range(0, len(jobs), ARRIVALS):
        products = []
        for k, (got, place) in enumerate(jobs[first : first + ARRIVALS]):
            at = first_slot + first + k
            matrix = circulant[pl.ds(starts[at], TILE), :].astype(jnp.bfloat16)
            tile = got[place]
            tile = jnp.where(scales[at] > 0.0, tile, jnp.zeros_like(tile))
            products.append(jnp.dot(tile, matrix, preferred_element_type=jnp.float32) * scales[at])
        for k, product in enumerate(products):
            target = targets[first_slot + first + k]
            total[target] = total[target] + product
    if total is not out:
        out[...] = total[...].astype(out.dtype)


def gathered(block, axis_name):
    peers = lax.axis_size(axis_name)
    step = 1
    while step < peers:
        other = lax.ppermute(block, axis_name, [(i, i ^ step) for i in range(peers)])
        block = jnp.concatenate([block, other], axis=0)
        step *= 2
    return block


def arrivals(owner, details, everything):
    senders, _, tile_count = details.shape
    slot_count = senders * CAP
    here = owner * CAP + jnp.arange(CAP, dtype=jnp.int32)
    match = (details[:, None, 0, :] == here[None, :, None]).reshape(slot_count, 1, tile_count)
    fields = jnp.repeat(details[:, 1:], CAP, axis=0).reshape(slot_count, 3, tile_count)
    chosen = jnp.sum(jnp.where(match, fields, 0), axis=2)
    map_iota = jnp.arange(MAP_DEV, dtype=jnp.int32)
    owned = jnp.where(everything[:, 0] // CAP == owner, everything[:, 3], 0).astype(jnp.float32)
    on_map = everything[:, 1][None] == map_iota[:, None, None]
    sums = jnp.sum(jnp.where(on_map, owned[None], 0.0), axis=(1, 2))
    inverse = 1.0 / jnp.maximum(sums, 1.0)
    picked = chosen[:, 0][:, None] == map_iota[None, :]
    scales = jnp.sum(jnp.where(picked, inverse[None, :], 0.0), axis=1) * chosen[:, 2].astype(jnp.float32)
    return chosen[:, 0], (TILE - chosen[:, 1]) & (TILE - 1), scales


def map_sum(lists, rounded_kernel, tiles, kind, name, first_slot, begun=()):
    extent = (MAP_DEV,) + tiles[0].shape[1:]
    scratch = [pltpu.VMEM((2 * TILE, TILE), jnp.float32)]
    if kind != jnp.float32:
        scratch.append(pltpu.VMEM(extent, jnp.float32))
    return pl.pallas_call(
        partial(map_kernel, arrays=len(tiles), first_slot=first_slot),
        out_shape=jax.ShapeDtypeStruct(extent, kind),
        in_specs=[SMEM] * 4 + [VMEM] * (len(tiles) + len(begun)),
        out_specs=VMEM,
        scratch_shapes=scratch,
        compiler_params=params,
        name=name,
    )(*lists, rounded_kernel, *tiles, *begun)


def shards(
    radar_stack,
    filter_taps,
    filter_lengths,
    resample_kernel,
    tile_owner,
    map_slot,
    correlation,
    offsets,
):
    peers = lax.axis_size("date")
    me = lax.axis_index("date")
    _, dates_here, rows_count, ranges_count = radar_stack.shape
    dates = dates_here * peers
    line_count = rows_count // peers
    sides = ranges_count // TILE
    tile_count = line_count * sides
    slot_count = peers * CAP
    window_count = (line_count // PATCH_AZ) * (ranges_count // PATCH_RG)
    assert line_count == PATCH_AZ

    sent = pl.pallas_call(
        filter_kernel,
        out_shape=pltpu.HBM((rows_count * 2 * dates_here, ranges_count), jnp.bfloat16),
        in_specs=[HBM, HBM, HBM],
        out_specs=HBM,
        scratch_shapes=[
            pltpu.SMEM((dates_here,), jnp.int32),
            pltpu.VMEM(filter_taps.shape, jnp.float32),
            pltpu.VMEM((dates_here, 2, rows_count, ranges_count), jnp.bfloat16),
            pltpu.VMEM((sides, rows_count * 2 * dates_here, TILE), jnp.float32),
            pltpu.VMEM((rows_count * 2 * dates_here, ranges_count), jnp.bfloat16),
            pltpu.SemaphoreType.DMA((dates_here + 2,)),
            pltpu.SemaphoreType.DMA((PIECES,)),
        ],
        compiler_params=wide_params,
        name="filter",
    )(filter_lengths, filter_taps, radar_stack)
    sent, tile_owner, map_slot, correlation, offsets, resample_kernel = lax.optimization_barrier(
        (sent, tile_owner, map_slot, correlation, offsets, resample_kernel)
    )
    owners = tile_owner[:, 0]
    tile_iota = jnp.arange(tile_count, dtype=jnp.int32)
    starts_here = offsets + PATCH_RG * (tile_iota // sides)
    earlier = jnp.logical_and(
        owners[:, None] == owners[None, :], tile_iota[None, :] < tile_iota[:, None]
    )
    half = peers // 2
    assert peers & (peers - 1) == 0
    ranks = jnp.sum(earlier, axis=1).astype(jnp.int32)
    step = (owners % half) ^ (me % half)
    leaves = owners // half != me // half
    chips = half // 2
    alone = jnp.logical_and(leaves, step % 2 == 0)
    slots = jnp.where(alone, 0, step // 2 * CAP) + ranks
    routes = jnp.where(alone, step // 2, chips + jnp.where(leaves, 0, 1 + step % 2))
    details = jnp.stack([owners * CAP + ranks, map_slot, starts_here, correlation], axis=0)[None]
    sent = sent.reshape(peers, line_count * 2 * dates_here, ranges_count)
    got_lines = lax.all_to_all(sent, "date", split_axis=0, concat_axis=0, tiled=True)
    all_details = gathered(details, "date")
    rounded_kernel = lax.optimization_barrier(resample_kernel.astype(jnp.bfloat16)).astype(jnp.float32)
    got_lines, all_details, rounded_kernel = lax.optimization_barrier(
        (got_lines, all_details, rounded_kernel)
    )

    mixed = dates_here == 8 and peers % 2 == 0
    got_lines = got_lines.reshape(peers, line_count, 2 * dates_here, ranges_count)
    if not mixed:
        got_lines = got_lines.reshape(peers, line_count, 2, dates_here, ranges_count)
        got_lines = got_lines.transpose(1, 2, 0, 3, 4).reshape(1, line_count, 2 * dates, ranges_count)
    buffer = pltpu.HBM((chips * CAP, 2 * dates, TILE), jnp.bfloat16)
    chip_buffer = pltpu.HBM((CAP, 2 * dates, TILE), jnp.bfloat16)
    *leaving_same, leaving_other, same, other = pl.pallas_call(
        partial(whiten_kernel, mixed=mixed),
        out_shape=(chip_buffer,) * chips + (buffer,) * 3,
        in_specs=[SMEM, SMEM, VMEM],
        out_specs=(HBM,) * (chips + 3),
        scratch_shapes=[
            pltpu.VMEM((window_count, 2 * dates, TILE), jnp.bfloat16),
            pltpu.VMEM((tile_count, 2 * dates, TILE), jnp.bfloat16),
            pltpu.SemaphoreType.DMA((tile_count,)),
        ],
        compiler_params=params,
        name="whiten",
    )(slots, routes, got_lines)

    def exchanged(values, step):
        return lax.ppermute(values, "date", [(i, i ^ step) for i in range(peers)])

    def by_chip(cells):
        return [cells[k * CAP : (k + 1) * CAP] for k in range(chips)]

    def from_chips(mine, received):
        tiles = []
        for k, both in enumerate(zip(mine, received)):
            tiles += [exchanged(cells, 2 * k) if k else cells for cells in both]
        return tiles

    early = half // 2
    early_slots = early * CAP
    received = exchanged(leaving_other, 1)
    far_tiles = from_chips(leaving_same, by_chip(received))
    other = exchanged(other, 1)
    other, all_details = lax.optimization_barrier((other, all_details))
    near = all_details[:half]
    far_lists = arrivals((me + half) % peers, near, all_details)
    near_lists = arrivals(me, near, all_details)
    far_begun = map_sum(far_lists, rounded_kernel, far_tiles[:early], jnp.float32, "far_early", 0)
    partial_sums = map_sum(
        far_lists, rounded_kernel, far_tiles[early:], jnp.bfloat16, "far_late", early_slots, [far_begun]
    )
    partial_sums, same, other, near_lists = lax.optimization_barrier(
        (partial_sums, same, other, near_lists)
    )
    from_far = lax.ppermute(partial_sums, "date", [(i, (i + half) % peers) for i in range(peers)])
    near_tiles = from_chips(by_chip(same), by_chip(other))
    near_begun = map_sum(near_lists, rounded_kernel, near_tiles[:early], jnp.float32, "near_early", 0)
    return map_sum(
        near_lists,
        rounded_kernel,
        near_tiles[early:],
        jnp.float32,
        "near_late",
        early_slots,
        [near_begun, from_far],
    )


def solution(mesh):
    in_specs = (
        P(None, "date", "grp", None),
        P(None, "date", None),
        P("date"),
        P(),
        P(("grp", "date"), None),
        P(("grp", "date")),
        P(("grp", "date")),
        P(("grp", "date")),
    )
    out_specs = P(("grp", "date"), None, None)
    return jax.shard_map(shards, mesh=mesh, in_specs=in_specs, out_specs=out_specs, check_vma=False)
```
